32 devices in a mesh: section: 16 (over z, y, core), dp: 2 (over x).
Axes of the slice: x: 2, y: 2, z: 4, core: 2. Of those that a mesh axis runs over, the one named last changes fastest.
Arguments:
- activations: bfloat16 [2, 16, 2, 8, 32, 416], P(None, 'section', 'dp'), may hold values from -6 to 6
- stored_inputs: bfloat16 [2, 3, 16, 2, 8, 32, 416], P(None, None, 'section', 'dp'), may hold values from -6 to 6
- cotangents: bfloat16 [2, 16, 2, 8, 32, 416], P(None, 'section', 'dp'), may hold values from -6 to 6
- new_inputs: bfloat16 [2, 2, 2, 8, 32, 416], P(None, None, 'dp'), may hold values from -6 to 6
- loss_grad: bfloat16 [2, 2, 2, 8, 32, 416], P(None, None, 'dp'), may hold values from -6 to 6
- depth_kernel: bfloat16 [16, 2, 1, 5, 5, 416], P('section'), may hold values from -1.25 to 1.25
- depth_bias: float32 [16, 2, 1, 416], P('section'), may hold values from -3 to 3
- mixing: bfloat16 [16, 2, 1, 416, 416], P('section'), may hold values from -0.3125 to 0.3125
Outputs:
- section_outputs: bfloat16 [2, 16, 2, 8, 32, 416], P(None, 'section', 'dp')
- input_grads: bfloat16 [2, 16, 2, 8, 32, 416], P(None, 'section', 'dp')
- grad_kernel: float32 [16, 1, 5, 5, 416], P('section', None, None, None, 'dp')
- grad_bias: float32 [16, 1, 416], P('section', None, 'dp')
- grad_mixing: float32 [16, 1, 416, 416], P('section', None, 'dp')
The draws below stay inside these ranges and needn't reach their ends.
All inputs are finite; a program needn't handle non-finite values.
Results may differ from the reference program's by a relative error of at most 0.0062.
Values may be sent and summed in bfloat16 or wider, within the bound.
A program may use at most 128 MiB of HBM per device.

```python
import jax
import jax.numpy as jnp
from jax import lax

C = 416
H = 8
W = 32
KS = 5
LAYERS = 1
TICKS = 3
SECTIONS = 16
IMGS = 2


def shard_levels(stream_key, shape, cuts, smallest, largest):
    gain, own = 1.0, jax.random.fold_in(stream_key, 6)
    for dim, shards_of in cuts:
        steps = jnp.exp(jax.random.uniform(jax.random.fold_in(own, dim), (shards_of,), jnp.float32, smallest / len(cuts), largest / len(cuts)))
        gain = gain * jnp.repeat(steps, shape[dim] // shards_of).reshape([-1 if axis == dim else 1 for axis in range(len(shape))])
    return gain


def gaussian(stream_key, shape, scale, most, pieces=(), held_as=jnp.bfloat16):
    values = scale * jax.random.normal(stream_key, shape, jnp.float32)
    if pieces:
        values = values * shard_levels(stream_key, shape, pieces, -0.22, 0.18)
    return jnp.clip(values, -most, most).astype(held_as)


def setup_inputs(seed: int = 0) -> dict:
    key_list = jax.random.split(jax.random.key(seed), 9)
    return {
        "activations": gaussian(key_list[0], (2, SECTIONS, IMGS, H, W, C), 1.0, 6.0, ((1, 16), (2, 2))),
        "stored_inputs": gaussian(key_list[1], (2, TICKS, SECTIONS, IMGS, H, W, C), 1.0, 6.0, ((2, 16), (3, 2))),
        "cotangents": gaussian(key_list[2], (2, SECTIONS, IMGS, H, W, C), 1.0, 6.0, ((1, 16), (2, 2))),
        "new_inputs": gaussian(key_list[3], (2, TICKS - 1, IMGS, H, W, C), 1.0, 6.0, ((2, 2),)),
        "loss_grad": gaussian(key_list[4], (2, TICKS - 1, IMGS, H, W, C), 1.0, 6.0, ((2, 2),)),
        "depth_kernel": gaussian(key_list[5], (SECTIONS, 2, LAYERS, KS, KS, C), (KS * KS) ** -0.5, 1.25, ((0, 16),)),
        "depth_bias": gaussian(key_list[6], (SECTIONS, 2, LAYERS, C), 0.5, 3.0, ((0, 16),), jnp.float32),
        "mixing": gaussian(key_list[7], (SECTIONS, 2, LAYERS, C, C), C ** -0.5, 0.3125, ((0, 16),)),
    }


def depthwise(maps_in, kernel):
    side = kernel.shape[0]
    margin = side // 2
    height = maps_in.shape[1]
    width = maps_in.shape[2]
    padded = jnp.pad(maps_in, ((0, 0), (margin, margin), (margin, margin), (0, 0)))
    running = jnp.zeros(maps_in.shape, maps_in.dtype)
    for tap_row in range(side):
        for tap_col in range(side):
            running = running + padded[:, tap_row:tap_row + height, tap_col:tap_col + width, :] * kernel[tap_row, tap_col]
    return running

def kernel_grad(maps_in, grad_pre, side):
    margin = side // 2
    height = maps_in.shape[1]
    width = maps_in.shape[2]
    padded = jnp.pad(maps_in, ((0, 0), (margin, margin), (margin, margin), (0, 0)))
    tap_list = []
    for tap_row in range(side):
        for tap_col in range(side):
            window = padded[:, tap_row:tap_row + height, tap_col:tap_col + width, :]
            tap_list.append(lax.optimization_barrier(jnp.sum(window * grad_pre, axis=(0, 1, 2))))
    return jnp.stack(tap_list).reshape(side, side, -1)

def layer_forward(maps_in, kernel, bias, mixing):
    channels = maps_in.shape[-1]
    pre_act = depthwise(maps_in.astype(jnp.float32), kernel.astype(jnp.float32)) + bias
    hidden = jax.nn.gelu(pre_act).astype(jnp.bfloat16)
    mixed_out = jnp.dot(hidden.reshape(-1, channels), mixing, preferred_element_type=jnp.float32)
    result = (maps_in.astype(jnp.float32) + mixed_out.reshape(maps_in.shape)).astype(jnp.bfloat16)
    return (pre_act, hidden, result)

def section_forward(maps_in, kernels, biases, mixings):
    for depth_pos in range(kernels.shape[0]):
        maps_in = layer_forward(maps_in, kernels[depth_pos], biases[depth_pos], mixings[depth_pos])[2]
    return maps_in

def section_backward(maps_in, incoming, kernels, biases, mixings):
    channels = maps_in.shape[-1]
    side = kernels.shape[1]
    stored = []
    for depth_pos in range(kernels.shape[0]):
        pre_act, hidden, result = layer_forward(maps_in, kernels[depth_pos], biases[depth_pos], mixings[depth_pos])
        stored.append((maps_in, pre_act, hidden))
        maps_in = result
    kernel_list = []
    bias_list = []
    mixing_list = []
    for depth_pos in reversed(range(kernels.shape[0])):
        layer_in, pre_act, hidden = stored[depth_pos]
        flat_cot = incoming.reshape(-1, channels)
        grad_mix = lax.dot_general(hidden.reshape(-1, channels), flat_cot, (((0,), (0,)), ((), ())), preferred_element_type=jnp.float32)
        back_hidden = lax.dot_general(flat_cot, mixings[depth_pos], (((1,), (1,)), ((), ())), preferred_element_type=jnp.float32).reshape(pre_act.shape)
        grad_pre = jax.vjp(jax.nn.gelu, pre_act)[1](back_hidden)[0]
        bias_list.insert(0, lax.optimization_barrier(jnp.sum(grad_pre, axis=(0, 1, 2))))
        kernel_list.insert(0, kernel_grad(layer_in.astype(jnp.float32), grad_pre, side))
        mixing_list.insert(0, grad_mix)
        flipped = kernels[depth_pos][::-1, ::-1].astype(jnp.float32)
        incoming = (incoming.astype(jnp.float32) + depthwise(grad_pre, flipped)).astype(jnp.bfloat16)
    return (incoming, jnp.stack(kernel_list), jnp.stack(bias_list), jnp.stack(mixing_list))

def reference(activations, stored_inputs, cotangents, new_inputs, loss_grad, depth_kernel, depth_bias, mixing):
    tick_count = stored_inputs.shape[1]
    outputs_all = []
    grads_all = []
    totals_all = []
    for replica in range(2):
        weights = (depth_kernel[:, replica], depth_bias[:, replica], mixing[:, replica])
        current = activations[replica]
        results = current
        for tick_num in range(tick_count):
            results = lax.map(lambda members: section_forward(*members), (current,) + weights)
            if tick_num < tick_count - 1:
                if replica == 0:
                    current = jnp.concatenate([new_inputs[0, tick_num][None], results[:-1]], 0)
                else:
                    current = jnp.concatenate([results[1:], new_inputs[1, tick_num][None]], 0)
        outputs_all.append(results)
        incoming = cotangents[replica]
        totals = None
        backed = None
        for tick_num in range(tick_count):
            backed = lax.map(lambda members: section_backward(*members), (stored_inputs[replica, tick_num], incoming) + weights)
            if totals is None:
                totals = backed[1:]
            else:
                totals = tuple((left + right for left, right in zip(totals, backed[1:])))
            if tick_num < tick_count - 1:
                if replica == 0:
                    incoming = jnp.concatenate([backed[0][1:], loss_grad[0, tick_num][None]], 0)
                else:
                    incoming = jnp.concatenate([loss_grad[1, tick_num][None], backed[0][:-1]], 0)
        grads_all.append(backed[0])
        totals_all.append(totals)
    factor = (2.0 * tick_count * activations.shape[2] * activations.shape[3] * activations.shape[4]) ** (-0.5)
    summed = tuple(((totals_all[0][j] + totals_all[1][j][::-1]) * factor for j in range(3)))
    return (jnp.stack(outputs_all), jnp.stack(grads_all), summed[0], summed[1], summed[2])
```

```python
import functools
import math

import jax
import jax.numpy as jnp
from jax import lax
from jax.experimental import pallas as pl
from jax.experimental.pallas import tpu as pltpu
from jax.sharding import PartitionSpec as P

LANES = 128
SUB = 8
GELU_A = math.sqrt(2.0 / math.pi)
GELU_B = GELU_A * 0.044715
MESH = pl.DeviceIdType.MESH


def relay_kernel(
    n, act, cot, new_in, loss, stored, kern, bias, mix,
    y_out, dx_out, dp_out, dk_out,
    xf, xb, dpad, hid, hidb, slope, work, kw, dk_acc, rx, tx,
    local_sem, send_sem, recv_sem, out_sem,
):
    ticks = stored.shape[1]
    height, width, chans = stored.shape[-3:]
    side = kern.shape[-2]
    margin = side // 2
    tiles = xf.shape[0]
    taps = side * side
    widths = [min(LANES, chans - t * LANES) for t in range(tiles)]
    pos = lax.axis_index("section")
    right, left = lax.rem(pos + 1, n), lax.rem(pos + n - 1, n)

    for c in range(4):
        first = (act if c < 2 else cot).at[c % 2, 0, 0]
        pltpu.make_async_copy(first, rx.at[0, c], local_sem.at[0, c]).start()
    for c, entry in ((0, 0), (1, n - 1), (2, n - 1), (3, 0)):
        @pl.when(pos == entry)
        def _():
            for t in range(1, ticks):
                source = (new_in if c < 2 else loss).at[c % 2, t - 1, 0]
                pltpu.make_async_copy(source, rx.at[t, c], local_sem.at[t, c]).start()

    barrier = pltpu.get_barrier_semaphore()
    for other in (left, right):
        pl.semaphore_signal(barrier, inc=1, device_id={"section": other}, device_id_type=MESH)

    xf[...] = jnp.zeros(xf.shape, jnp.float32)
    xb[...] = jnp.zeros(xb.shape, jnp.float32)
    dpad[...] = jnp.zeros(dpad.shape, jnp.float32)
    dk_acc[...] = jnp.zeros(dk_acc.shape, jnp.float32)
    dp_out[...] = jnp.zeros(dp_out.shape, jnp.float32)
    kw[...] = jnp.zeros(kw.shape, jnp.float32)
    for r in range(2):
        for l, wide in enumerate(widths):
            lanes = slice(l * LANES, l * LANES + wide)
            for a in range(side):
                kw[r, l, a * side : (a + 1) * side, :wide] = kern[0, r, 0, a, :, lanes].astype(jnp.float32)
            kw[r, l, taps : taps + 1, :wide] = bias[0, r, :, lanes]
    pl.semaphore_wait(barrier, 2)

    def stage(source, dest):
        for l, wide in enumerate(widths):
            values = source[:, :, l * LANES : l * LANES + wide].astype(jnp.float32)
            dest[l, :, SUB : SUB + width, :wide] = values

    def shifted(ref, h, b):
        start = SUB - margin + b
        return ref[h, start : start + width, :]

    def conv(ref, r, l, flip, init):
        total = [init] * height
        for b in range(side):
            row = []
            for a in range(side):
                place = taps - 1 - (a * side + b) if flip else a * side + b
                row.append(jnp.broadcast_to(kw[r, l, place : place + 1, :], (width, LANES)))
            for source in range(height):
                values = shifted(ref, source, b)
                for a in range(side):
                    h = source - a + margin
                    if 0 <= h < height:
                        total[h] = total[h] + values * row[a]
        return total

    def rows(h):
        return pl.ds(h * width, width)

    def lane_tile(l):
        return pl.ds(pl.multiple_of(l * LANES, LANES), LANES)

    def link(t, c, dst):
        return pltpu.make_async_remote_copy(
            src_ref=tx.at[t, c],
            dst_ref=rx.at[t + 1, c],
            send_sem=send_sem.at[t, c],
            recv_sem=recv_sem.at[t + 1, c],
            device_id={"section": dst},
            device_id_type=MESH,
        )

    def inside(place):
        return jnp.logical_and(place >= 0, place < n)

    def arrive(t, c, src):
        remote = jnp.logical_and(t > 0, inside(src))

        @pl.when(remote)
        def _():
            pltpu.make_async_remote_copy(
                src_ref=tx.at[t, c],
                dst_ref=rx.at[t, c],
                send_sem=send_sem.at[t, c],
                recv_sem=recv_sem.at[t, c],
                device_id={"section": left},
                device_id_type=MESH,
            ).wait_recv()

        @pl.when(jnp.logical_not(remote))
        def _():
            pltpu.make_async_copy(act.at[0, 0, 0], rx.at[t, c], local_sem.at[t, c]).wait()

    def depart(t, c, dst):
        @pl.when(jnp.logical_and(t < ticks - 1, inside(dst)))
        def _():
            link(t, c, dst).start()

    def forward(r, t):
        arrive(t, r, pos - 1 + 2 * r)
        stage(rx.at[t, r], xf)

        def tile(l, carry):
            first = jnp.broadcast_to(kw[r, l, taps : taps + 1, :], (width, LANES))
            total = conv(xf.at[l], r, l, False, first)
            for h in range(height):
                u = total[h]
                half = 0.5 * u
                th = jnp.tanh(u * (GELU_A + GELU_B * (u * u)))
                hid[rows(h), lane_tile(l)] = (half + half * th).astype(jnp.bfloat16)
            return carry

        lax.fori_loop(0, tiles, tile, 0)
        mixed = jnp.dot(hid[:, :chans], mix[0, r, 0], preferred_element_type=jnp.float32)
        result = rx[t, r].astype(jnp.float32) + mixed.reshape(height, width, chans)
        tx[t, r] = result.astype(jnp.bfloat16)
        depart(t, r, pos + 1 - 2 * r)

    def backward(r, t):
        stage(stored.at[r, t, 0, 0], xb.at[r])

        def tile(l, carry):
            first = jnp.broadcast_to(kw[r, l, taps : taps + 1, :], (width, LANES))
            total = conv(xb.at[r, l], r, l, False, first)
            for h in range(height):
                u = total[h]
                half = 0.5 * u
                square = u * u
                th = jnp.tanh(u * (GELU_A + GELU_B * square))
                hidb[r, rows(h), lane_tile(l)] = (half + half * th).astype(jnp.bfloat16)
                inner = GELU_A + (3.0 * GELU_B) * square
                slope[l, rows(h), :] = (0.5 + 0.5 * th) + half * (1.0 - th * th) * inner
            return carry

        lax.fori_loop(0, tiles, tile, 0)
        arrive(t, 2 + r, pos + 1 - 2 * r)
        incoming = rx[t, 2 + r].reshape(height * width, chans)
        work[:, :chans] = lax.dot_general(
            incoming, mix[0, r, 0], (((1,), (1,)), ((), ())), preferred_element_type=jnp.float32
        )

        def spread(l, carry):
            bias_sum = jnp.zeros((SUB, LANES), jnp.float32)
            for h in range(height):
                grad = work[rows(h), lane_tile(l)] * slope[l, rows(h), :]
                dpad[r, l, h, SUB : SUB + width, :] = grad
                for w in range(0, width, SUB):
                    bias_sum = bias_sum + grad[w : w + SUB]
            dk_acc[r, l, taps] = dk_acc[r, l, taps] + bias_sum
            total = conv(dpad.at[r, l], r, l, True, jnp.zeros((width, LANES), jnp.float32))
            for h in range(height):
                work[rows(h), lane_tile(l)] = total[h]
            return carry

        lax.fori_loop(0, tiles, spread, 0)
        result = rx[t, 2 + r].astype(jnp.float32) + work[:, :chans].reshape(height, width, chans)
        tx[t, 2 + r] = result.astype(jnp.bfloat16)
        depart(t, 2 + r, pos - 1 + 2 * r)

    def weights(r, t):
        incoming = rx[t, 2 + r].reshape(height * width, chans)
        dp_out[r] += lax.dot_general(
            hidb[r, :, :chans], incoming, (((0,), (0,)), ((), ())), preferred_element_type=jnp.float32
        )

        def tile(l, carry):
            grads = [dpad[r, l, h, SUB : SUB + width, :] for h in range(height)]
            for b in range(side):
                sums = [None] * side
                for source in range(height):
                    values = shifted(xb.at[r, l], source, b)
                    for a in range(side):
                        h = source - a + margin
                        if 0 <= h < height:
                            product = grads[h] * values
                            for w in range(0, width, SUB):
                                part = product[w : w + SUB]
                                sums[a] = part if sums[a] is None else sums[a] + part
                for a in range(side):
                    dk_acc[r, l, a * side + b] = dk_acc[r, l, a * side + b] + sums[a]
            return carry

        lax.fori_loop(0, tiles, tile, 0)

    def over_replicas(step, t):
        def one(r, carry):
            step(r, t)
            return carry

        lax.fori_loop(0, 2, one, 0)

    def tick(t, carry):
        over_replicas(forward, t)
        over_replicas(backward, t)
        over_replicas(weights, t)
        return carry

    lax.fori_loop(0, ticks, tick, 0)

    outs = []
    for c in range(4):
        target = (y_out if c < 2 else dx_out).at[c % 2, 0, 0]
        copy = pltpu.make_async_copy(tx.at[ticks - 1, c], target, out_sem.at[c])
        copy.start()
        outs.append(copy)
    for r in range(2):
        for l, wide in enumerate(widths):
            total = jnp.sum(dk_acc[r, l], axis=1)
            dk_out[r, : taps + 1, l * LANES : l * LANES + wide] = total[:, :wide]
    for t in range(ticks - 1):
        for c, step in ((0, 1), (1, -1), (2, -1), (3, 1)):
            @pl.when(inside(pos + step))
            def _():
                link(t, c, pos + step).wait_send()
    for copy in outs:
        copy.wait()


def relay(n, act, cot, new_in, loss, stored, kern, bias, mix):
    ticks = stored.shape[1]
    height, width, chans = stored.shape[-3:]
    side = kern.shape[-2]
    taps = side * side
    tiles = -(-chans // LANES)
    padded = tiles * LANES
    count = height * width
    across = width + 2 * SUB
    f32, bf16 = jnp.float32, jnp.bfloat16
    vmem = pl.BlockSpec(memory_space=pltpu.VMEM)
    anywhere = pl.BlockSpec(memory_space=pl.ANY)
    small = -(-(taps + 1) // SUB) * SUB
    return pl.pallas_call(
        functools.partial(relay_kernel, n),
        out_shape=(
            jax.ShapeDtypeStruct(act.shape, bf16),
            jax.ShapeDtypeStruct(cot.shape, bf16),
            jax.ShapeDtypeStruct((2, chans, chans), f32),
            jax.ShapeDtypeStruct((2, taps + 1, chans), f32),
        ),
        in_specs=[anywhere] * 4 + [vmem] * 4,
        out_specs=(anywhere, anywhere, vmem, vmem),
        scratch_shapes=[
            pltpu.VMEM((tiles, height, across, LANES), f32),
            pltpu.VMEM((2, tiles, height, across, LANES), f32),
            pltpu.VMEM((2, tiles, height, across, LANES), f32),
            pltpu.VMEM((count, padded), bf16),
            pltpu.VMEM((2, count, padded), bf16),
            pltpu.VMEM((tiles, count, LANES), f32),
            pltpu.VMEM((count, padded), f32),
            pltpu.VMEM((2, tiles, small, LANES), f32),
            pltpu.VMEM((2, tiles, taps + 1, SUB, LANES), f32),
            pltpu.VMEM((ticks, 4, height, width, chans), bf16),
            pltpu.VMEM((ticks, 4, height, width, chans), bf16),
            pltpu.SemaphoreType.DMA((ticks, 4)),
            pltpu.SemaphoreType.DMA((ticks, 4)),
            pltpu.SemaphoreType.DMA((ticks, 4)),
            pltpu.SemaphoreType.DMA((4,)),
        ],
        compiler_params=pltpu.CompilerParams(
            collective_id=0, has_side_effects=True, vmem_limit_bytes=40 * 1024 * 1024
        ),
        name="relay",
    )(act, cot, new_in, loss, stored, kern, bias, mix)


def per_device(
    activations, stored_inputs, cotangents, new_inputs, loss_grad, depth_kernel, depth_bias, mixing
):
    sections = lax.axis_size("section")
    side = depth_kernel.shape[-2]
    taps = side * side
    ticks = stored_inputs.shape[1]
    outputs, grads, mix_sums, small_sums = relay(
        sections, activations, cotangents, new_inputs, loss_grad,
        stored_inputs, depth_kernel, depth_bias, mixing,
    )
    mix_share = lax.psum_scatter(mix_sums, "dp", scatter_dimension=1, tiled=True)
    small_share = lax.psum_scatter(small_sums, "dp", scatter_dimension=2, tiled=True)
    swap = [(i, sections - 1 - i) for i in range(sections)]
    mix_other, small_other = lax.ppermute((mix_share[1], small_share[1]), "section", swap)
    map_rows = activations.shape[3] * activations.shape[4]
    factor = (2.0 * ticks * activations.shape[2] * lax.axis_size("dp") * map_rows) ** (-0.5)
    grad_mixing = ((mix_share[0] + mix_other) * factor)[None, None]
    small = (small_share[0] + small_other) * factor
    grad_kernel = small[:taps].reshape(1, 1, side, side, -1)
    grad_bias = small[taps][None, None]
    return (outputs, grads, grad_kernel, grad_bias, grad_mixing)


def solution(mesh):
    return jax.shard_map(
        per_device,
        mesh=mesh,
        in_specs=(
            P(None, "section", "dp", None, None, None),
            P(None, None, "section", "dp", None, None, None),
            P(None, "section", "dp", None, None, None),
            P(None, None, "dp", None, None, None),
            P(None, None, "dp", None, None, None),
            P("section", None, None, None, None, None),
            P("section", None, None, None),
            P("section", None, None, None, None),
        ),
        out_specs=(
            P(None, "section", "dp", None, None, None),
            P(None, "section", "dp", None, None, None),
            P("section", None, None, None, "dp"),
            P("section", None, "dp"),
            P("section", None, "dp", None),
        ),
        check_vma=False,
    )
```

```python
import functools
import math

import jax
import jax.numpy as jnp
from jax import lax
from jax.experimental import pallas as pl
from jax.experimental.pallas import tpu as pltpu
from jax.sharding import PartitionSpec as P

LANES = 128
SUB = 8
GELU_A = math.sqrt(2.0 / math.pi)
GELU_B = GELU_A * 0.044715
MESH = pl.DeviceIdType.MESH


def relay_kernel(
    n, share, factor, act, cot, new_in, loss, stored_in, kern_in, bias_in, mix_in, *refs
):
    outs, refs = refs[:4 + (share > 0)], refs[4 + (share > 0):]
    y_out, dx_out = outs[:2]
    (
        xf, xb, dpad, hid, hidb, slope, work, kw, dk_acc, dp_acc, small, rx, tx,
        stored, kern, bias, mix, parcel, landed,
        local_sem, send_sem, recv_sem, out_sem, load_sem, stored_sem, swap_send, swap_recv,
    ) = refs
    ticks = stored.shape[1]
    height, width, chans = stored.shape[-3:]
    side = kern.shape[2]
    margin = side // 2
    tiles = xf.shape[0]
    taps = side * side
    widths = [min(LANES, chans - t * LANES) for t in range(tiles)]
    pos = lax.axis_index("section")
    right, left = lax.rem(pos + 1, n), lax.rem(pos + n - 1, n)

    loads = [
        pltpu.make_async_copy(source, dest, load_sem.at[i])
        for i, (source, dest) in enumerate(((kern_in, kern), (bias_in, bias), (mix_in, mix)))
    ]
    for load in loads:
        load.start()
    pltpu.make_async_copy(stored_in.at[1, 0], stored.at[1, 0], stored_sem.at[1, 0]).start()
    for c in range(4):
        first = (act if c < 2 else cot).at[c % 2, 0, 0]
        pltpu.make_async_copy(first, rx.at[0, c], local_sem.at[0, c]).start()
    for t in range(ticks):
        for r in (1, 0):
            if (r, t) != (1, 0):
                pltpu.make_async_copy(stored_in.at[r, t], stored.at[r, t], stored_sem.at[r, t]).start()
    for c, entry in ((0, 0), (1, n - 1), (2, n - 1), (3, 0)):
        @pl.when(pos == entry)
        def _():
            for t in range(1, ticks):
                source = (new_in if c < 2 else loss).at[c % 2, t - 1, 0]
                pltpu.make_async_copy(source, rx.at[t, c], local_sem.at[t, c]).start()

    barrier = pltpu.get_barrier_semaphore()
    greeted = [{"section": left}, {"section": right}]
    if share:
        half = lax.axis_index("dp")
        peer, mirror = {"dp": 1 - half}, {"section": n - 1 - pos}
        greeted += [peer, mirror]
    for other in greeted:
        pl.semaphore_signal(barrier, inc=1, device_id=other, device_id_type=MESH)

    for ref in (xf, xb, dpad):
        edge = jnp.zeros(ref.shape[:-2] + (SUB, LANES), jnp.float32)
        ref[..., :SUB, :] = edge
        ref[..., SUB + width :, :] = edge
    dk_acc[...] = jnp.zeros(dk_acc.shape, jnp.float32)
    dp_acc[...] = jnp.zeros(dp_acc.shape, jnp.float32)
    small[...] = jnp.zeros(small.shape, jnp.float32)
    for load in loads:
        load.wait()
    for a in range(side):
        for b in range(side):
            pair = kern[0, 0, a, b].astype(jnp.float32)
            place = a * side + b
            for l, wide in enumerate(widths):
                for r in range(2):
                    kw[r, l, place : place + 1, :wide] = pair[r : r + 1, l * LANES : l * LANES + wide]
    for l, wide in enumerate(widths):
        for r in range(2):
            kw[r, l, taps : taps + 1, :wide] = bias[0, r, :, l * LANES : l * LANES + wide]
    pl.semaphore_wait(barrier, len(greeted))

    def stage(source, dest):
        for l, wide in enumerate(widths):
            values = source[:, :, l * LANES : l * LANES + wide].astype(jnp.float32)
            dest[l, :, SUB : SUB + width, :wide] = values

    def shifted(ref, h, b):
        start = SUB - margin + b
        return ref[h, start : start + width, :]

    def conv(ref, r, l, flip, init):
        total = [init] * height
        for b in range(side):
            row = []
            for a in range(side):
                place = taps - 1 - (a * side + b) if flip else a * side + b
                row.append(jnp.broadcast_to(kw[r, l, place : place + 1, :], (width, LANES)))
            for source in range(height):
                values = shifted(ref, source, b)
                for a in range(side):
                    h = source - a + margin
                    if 0 <= h < height:
                        total[h] = total[h] + values * row[a]
        return total

    def rows(h):
        return pl.ds(h * width, width)

    def lane_tile(l):
        return pl.ds(pl.multiple_of(l * LANES, LANES), LANES)

    def link(t, c, dst):
        return pltpu.make_async_remote_copy(
            src_ref=tx.at[t, c],
            dst_ref=rx.at[t + 1, c],
            send_sem=send_sem.at[t, c],
            recv_sem=recv_sem.at[t + 1, c],
            device_id={"section": dst},
            device_id_type=MESH,
        )

    def inside(place):
        return jnp.logical_and(place >= 0, place < n)

    def arrive(t, c, src):
        remote = jnp.logical_and(t > 0, inside(src))

        @pl.when(remote)
        def _():
            pltpu.make_async_remote_copy(
                src_ref=tx.at[t, c],
                dst_ref=rx.at[t, c],
                send_sem=send_sem.at[t, c],
                recv_sem=recv_sem.at[t, c],
                device_id={"section": left},
                device_id_type=MESH,
            ).wait_recv()

        @pl.when(jnp.logical_not(remote))
        def _():
            pltpu.make_async_copy(act.at[0, 0, 0], rx.at[t, c], local_sem.at[t, c]).wait()

    def depart(t, c, dst):
        @pl.when(jnp.logical_and(t < ticks - 1, inside(dst)))
        def _():
            link(t, c, dst).start()

    def forward(r, t):
        arrive(t, r, pos - 1 + 2 * r)
        stage(rx.at[t, r], xf)

        def tile(l, carry):
            first = jnp.broadcast_to(kw[r, l, taps : taps + 1, :], (width, LANES))
            total = conv(xf.at[l], r, l, False, first)
            for h in range(height):
                u = total[h]
                half = 0.5 * u
                th = jnp.tanh(u * (GELU_A + GELU_B * (u * u)))
                hid[rows(h), lane_tile(l)] = (half + half * th).astype(jnp.bfloat16)
            return carry

        lax.fori_loop(0, tiles, tile, 0)
        mixed = jnp.dot(hid[:, :chans], mix[0, r, 0], preferred_element_type=jnp.float32)
        result = rx[t, r].astype(jnp.float32) + mixed.reshape(height, width, chans)
        tx[t, r] = result.astype(jnp.bfloat16)
        depart(t, r, pos + 1 - 2 * r)

    def backward(r, t):
        pltpu.make_async_copy(stored_in.at[r, t], stored.at[r, t], stored_sem.at[r, t]).wait()
        stage(stored.at[r, t, 0, 0], xb.at[r])

        def tile(l, carry):
            first = jnp.broadcast_to(kw[r, l, taps : taps + 1, :], (width, LANES))
            total = conv(xb.at[r, l], r, l, False, first)
            for h in range(height):
                u = total[h]
                half = 0.5 * u
                square = u * u
                th = jnp.tanh(u * (GELU_A + GELU_B * square))
                hidb[r, rows(h), lane_tile(l)] = (half + half * th).astype(jnp.bfloat16)
                inner = GELU_A + (3.0 * GELU_B) * square
                slope[l, rows(h), :] = (0.5 + 0.5 * th) + half * (1.0 - th * th) * inner
            return carry

        lax.fori_loop(0, tiles, tile, 0)
        arrive(t, 2 + r, pos + 1 - 2 * r)
        incoming = rx[t, 2 + r].reshape(height * width, chans)
        work[:, :chans] = lax.dot_general(
            incoming, mix[0, r, 0], (((1,), (1,)), ((), ())), preferred_element_type=jnp.float32
        )

        def spread(l, carry):
            bias_sum = jnp.zeros((SUB, LANES), jnp.float32)
            for h in range(height):
                grad = work[rows(h), lane_tile(l)] * slope[l, rows(h), :]
                dpad[r, l, h, SUB : SUB + width, :] = grad
                for w in range(0, width, SUB):
                    bias_sum = bias_sum + grad[w : w + SUB]
            dk_acc[r, l, taps] = dk_acc[r, l, taps] + bias_sum
            total = conv(dpad.at[r, l], r, l, True, jnp.zeros((width, LANES), jnp.float32))
            for h in range(height):
                work[rows(h), lane_tile(l)] = total[h]
            return carry

        lax.fori_loop(0, tiles, spread, 0)
        result = rx[t, 2 + r].astype(jnp.float32) + work[:, :chans].reshape(height, width, chans)
        tx[t, 2 + r] = result.astype(jnp.bfloat16)
        depart(t, 2 + r, pos - 1 + 2 * r)

    def weights(r, t):
        incoming = rx[t, 2 + r].reshape(height * width, chans)
        dp_acc[r] += lax.dot_general(
            hidb[r, :, :chans], incoming, (((0,), (0,)), ((), ())), preferred_element_type=jnp.float32
        )

        def tile(l, carry):
            grads = [dpad[r, l, h, SUB : SUB + width, :] for h in range(height)]
            for b in range(side):
                sums = [None] * side
                for source in range(height):
                    values = shifted(xb.at[r, l], source, b)
                    for a in range(side):
                        h = source - a + margin
                        if 0 <= h < height:
                            product = grads[h] * values
                            for w in range(0, width, SUB):
                                part = product[w : w + SUB]
                                sums[a] = part if sums[a] is None else sums[a] + part
                for a in range(side):
                    dk_acc[r, l, a * side + b] = dk_acc[r, l, a * side + b] + sums[a]
            return carry

        lax.fori_loop(0, tiles, tile, 0)

    def finish_small(r):
        for l, wide in enumerate(widths):
            total = jnp.sum(dk_acc[r, l], axis=1)
            small[r, : taps + 1, l * LANES : l * LANES + wide] = total[:, :wide]

    if share:
        swaps = [
            pltpu.make_async_remote_copy(
                src_ref=parcel.at[i],
                dst_ref=landed.at[i],
                send_sem=swap_send.at[i],
                recv_sem=swap_recv.at[i],
                device_id=mirror if i == 2 else peer,
                device_id_type=MESH,
            )
            for i in range(3)
        ]

    def mix_half(r, which):
        return dp_acc[r, pl.ds(pl.multiple_of(which * share, SUB), share), :]

    def small_half(r, which):
        return jnp.where(which == 0, small[r, :, :share], small[r, :, share:])

    def send_half(r):
        finish_small(r)
        parcel[r, :share, :] = mix_half(r, 1 - half).astype(jnp.bfloat16)
        parcel[r, share:, :share] = small_half(r, 1 - half).astype(jnp.bfloat16)
        swaps[r].start()

    def send_mirror():
        swaps[1].wait_recv()
        mixed = mix_half(1, half) + landed[1, :share, :].astype(jnp.float32)
        parcel[2, :share, :] = mixed.astype(jnp.bfloat16)
        rest = small_half(1, half) + landed[1, share:, :share].astype(jnp.float32)
        parcel[2, share:, :share] = rest.astype(jnp.bfloat16)
        swaps[2].start()

    def tick(t, carry):
        last = t == ticks - 1
        for r in (1, 0):
            backward(r, t)
            if share and r == 0:
                pl.when(last)(send_mirror)
            weights(r, t)
            if share:
                pl.when(last)(functools.partial(send_half, r))
        for r in (0, 1):
            forward(r, t)
        return carry

    lax.fori_loop(0, ticks, tick, 0)

    done = []
    for c in range(4):
        target = (y_out if c < 2 else dx_out).at[c % 2, 0, 0]
        copy = pltpu.make_async_copy(tx.at[ticks - 1, c], target, out_sem.at[c])
        copy.start()
        done.append(copy)
    for t in range(ticks - 1):
        for c, step in ((0, 1), (1, -1), (2, -1), (3, 1)):
            @pl.when(inside(pos + step))
            def _():
                link(t, c, pos + step).wait_send()
    if share:
        gm_out, gk_out, gb_out = outs[2:]
        swaps[0].wait_recv()
        swaps[2].wait_recv()
        mixed = mix_half(0, half) + landed[0, :share, :].astype(jnp.float32)
        gm_out[0, 0] = (mixed + landed[2, :share, :].astype(jnp.float32)) * factor
        rest = small_half(0, half) + landed[0, share:, :share].astype(jnp.float32)
        rest = (rest + landed[2, share:, :share].astype(jnp.float32)) * factor
        for a in range(side):
            gk_out[0, 0, a] = rest[a * side : (a + 1) * side]
        gb_out[0] = rest[taps : taps + 1]
        for swap in swaps:
            swap.wait_send()
    else:
        for r in range(2):
            finish_small(r)
        outs[2][...] = dp_acc[...]
        outs[3][...] = small[...]
    for copy in done:
        copy.wait()


def relay(n, share, factor, act, cot, new_in, loss, stored, kern, bias, mix):
    ticks = stored.shape[1]
    height, width, chans = stored.shape[-3:]
    side = kern.shape[2]
    taps = side * side
    tiles = -(-chans // LANES)
    padded = tiles * LANES
    count = height * width
    across = width + 2 * SUB
    f32, bf16 = jnp.float32, jnp.bfloat16
    vmem = pl.BlockSpec(memory_space=pltpu.VMEM)
    anywhere = pl.BlockSpec(memory_space=pl.ANY)
    small = -(-(taps + 1) // 16) * 16
    if share:
        sums = [(1, 1, share, chans), (1, 1, side, side, share), (1, 1, share)]
    else:
        sums = [(2, chans, chans), (2, small, chans)]
    return pl.pallas_call(
        functools.partial(relay_kernel, n, share, factor),
        out_shape=(
            jax.ShapeDtypeStruct(act.shape, bf16),
            jax.ShapeDtypeStruct(cot.shape, bf16),
            *(jax.ShapeDtypeStruct(shape, f32) for shape in sums),
        ),
        in_specs=[anywhere] * 8,
        out_specs=(anywhere, anywhere, *(vmem for _ in sums)),
        scratch_shapes=[
            pltpu.VMEM((tiles, height, across, LANES), f32),
            pltpu.VMEM((2, tiles, height, across, LANES), f32),
            pltpu.VMEM((2, tiles, height, across, LANES), f32),
            pltpu.VMEM((count, padded), bf16),
            pltpu.VMEM((2, count, padded), bf16),
            pltpu.VMEM((tiles, count, LANES), f32),
            pltpu.VMEM((count, padded), f32),
            pltpu.VMEM((2, tiles, small, LANES), f32),
            pltpu.VMEM((2, tiles, taps + 1, SUB, LANES), f32),
            pltpu.VMEM((2, chans, chans), f32),
            pltpu.VMEM((2, small, chans), f32),
            pltpu.VMEM((ticks, 4, height, width, chans), bf16),
            pltpu.VMEM((ticks, 4, height, width, chans), bf16),
            pltpu.VMEM(stored.shape, bf16),
            pltpu.VMEM(kern.shape, bf16),
            pltpu.VMEM(bias.shape, f32),
            pltpu.VMEM(mix.shape, bf16),
            pltpu.VMEM((3, share + small, chans), bf16),
            pltpu.VMEM((3, share + small, chans), bf16),
            pltpu.SemaphoreType.DMA((ticks, 4)),
            pltpu.SemaphoreType.DMA((ticks, 4)),
            pltpu.SemaphoreType.DMA((ticks, 4)),
            pltpu.SemaphoreType.DMA((4,)),
            pltpu.SemaphoreType.DMA((3,)),
            pltpu.SemaphoreType.DMA((2, ticks)),
            pltpu.SemaphoreType.DMA((3,)),
            pltpu.SemaphoreType.DMA((3,)),
        ],
        compiler_params=pltpu.CompilerParams(
            collective_id=0, has_side_effects=True, vmem_limit_bytes=60 * 1024 * 1024
        ),
        name="relay",
    )(act, cot, new_in, loss, stored, kern, bias, mix)


def per_device(
    activations, stored_inputs, cotangents, new_inputs, loss_grad, depth_kernel, depth_bias, mixing
):
    sections = lax.axis_size("section")
    copies = lax.axis_size("dp")
    side = depth_kernel.shape[-2]
    taps = side * side
    ticks = stored_inputs.shape[1]
    chans = mixing.shape[-1]
    map_rows = activations.shape[3] * activations.shape[4]
    factor = (2.0 * ticks * activations.shape[2] * copies * map_rows) ** (-0.5)
    in_kernel = copies == 2 and sections % 2 == 0 and chans % 32 == 0
    share = chans // 2 if in_kernel else 0
    outputs, grads, *sums = relay(
        sections, share, factor, activations, cotangents, new_inputs, loss_grad,
        stored_inputs, depth_kernel.transpose(0, 2, 3, 4, 1, 5), depth_bias, mixing,
    )
    if in_kernel:
        return (outputs, grads, sums[1], sums[2], sums[0])
    mix_share = lax.psum_scatter(sums[0], "dp", scatter_dimension=1, tiled=True)
    small_share = lax.psum_scatter(sums[1], "dp", scatter_dimension=2, tiled=True)
    swap = [(i, sections - 1 - i) for i in range(sections)]
    mix_other, small_other = lax.ppermute((mix_share[1], small_share[1]), "section", swap)
    grad_mixing = ((mix_share[0] + mix_other) * factor)[None, None]
    small = (small_share[0] + small_other) * factor
    grad_kernel = small[:taps].reshape(1, 1, side, side, -1)
    grad_bias = small[taps][None, None]
    return (outputs, grads, grad_kernel, grad_bias, grad_mixing)


def solution(mesh):
    return jax.shard_map(
        per_device,
        mesh=mesh,
        in_specs=(
            P(None, "section", "dp", None, None, None),
            P(None, None, "section", "dp", None, None, None),
            P(None, "section", "dp", None, None, None),
            P(None, None, "dp", None, None, None),
            P(None, None, "dp", None, None, None),
            P("section", None, None, None, None, None),
            P("section", None, None, None),
            P("section", None, None, None, None),
        ),
        out_specs=(
            P(None, "section", "dp", None, None, None),
            P(None, "section", "dp", None, None, None),
            P("section", None, None, None, "dp"),
            P("section", None, "dp"),
            P("section", None, "dp", None),
        ),
        check_vma=False,
    )
```

```python
import functools
import math

import jax
import jax.numpy as jnp
from jax import lax
from jax.experimental import pallas as pl
from jax.experimental.pallas import tpu as pltpu
from jax.sharding import PartitionSpec as P

LANES = 128
SUB = 8
GELU_A = math.sqrt(2.0 / math.pi)
GELU_B = GELU_A * 0.044715
MESH = pl.DeviceIdType.MESH


def relay_kernel(
    n, share, factor, act, cot, new_in, loss, stored_in, kern_in, bias_in, mix_in, *refs
):
    outs, refs = refs[:4 + (share > 0)], refs[4 + (share > 0):]
    y_out, dx_out = outs[:2]
    (
        xf, xb, dpad, hid, hidb, hidden_grad, work, kw, dk_acc, dp_acc, small, rx, tx,
        stored, kern, bias, mix, parcel, landed,
        local_sem, send_sem, recv_sem, out_sem, load_sem, stored_sem, swap_send, swap_recv,
    ) = refs
    ticks = stored.shape[1]
    height, width, chans = stored.shape[-3:]
    side = kern.shape[2]
    margin = side // 2
    tiles = xf.shape[0]
    taps = side * side
    widths = [min(LANES, chans - t * LANES) for t in range(tiles)]
    pos = lax.axis_index("section")
    right, left = lax.rem(pos + 1, n), lax.rem(pos + n - 1, n)

    loads = [
        pltpu.make_async_copy(source, dest, load_sem.at[i])
        for i, (source, dest) in enumerate(
            ((kern_in, kern), (bias_in, bias), (mix_in.at[0, :, 0], mix.at[:, :chans]))
        )
    ]
    for load in loads:
        load.start()
    pltpu.make_async_copy(stored_in.at[1, 0], stored.at[1, 0], stored_sem.at[1, 0]).start()
    for c in range(4):
        first = (act if c < 2 else cot).at[c % 2, 0, 0]
        pltpu.make_async_copy(first, rx.at[0, c], local_sem.at[0, c]).start()
    for t in range(ticks):
        for r in (1, 0):
            if (r, t) != (1, 0):
                pltpu.make_async_copy(stored_in.at[r, t], stored.at[r, t], stored_sem.at[r, t]).start()
    for c, entry in ((0, 0), (1, n - 1), (2, n - 1), (3, 0)):
        @pl.when(pos == entry)
        def _():
            for t in range(1, ticks):
                source = (new_in if c < 2 else loss).at[c % 2, t - 1, 0]
                pltpu.make_async_copy(source, rx.at[t, c], local_sem.at[t, c]).start()

    barrier = pltpu.get_barrier_semaphore()
    greeted = [{"section": left}, {"section": right}]
    if share:
        half = lax.axis_index("dp")
        peer, mirror = {"dp": 1 - half}, {"section": n - 1 - pos}
        greeted += [peer, mirror]
    for other in greeted:
        pl.semaphore_signal(barrier, inc=1, device_id=other, device_id_type=MESH)

    for ref in (xf, xb, dpad):
        edge = jnp.zeros(ref.shape[:-2] + (SUB, LANES), jnp.float32)
        ref[..., :SUB, :] = edge
        ref[..., SUB + width :, :] = edge
    dk_acc[...] = jnp.zeros(dk_acc.shape, jnp.float32)
    dp_acc[...] = jnp.zeros(dp_acc.shape, jnp.float32)
    small[...] = jnp.zeros(small.shape, jnp.float32)
    for load in loads:
        load.wait()
    for a in range(side):
        for b in range(side):
            pair = kern[0, 0, a, b].astype(jnp.float32)
            place = a * side + b
            for l, wide in enumerate(widths):
                for r in range(2):
                    kw[r, l, place : place + 1, :wide] = pair[r : r + 1, l * LANES : l * LANES + wide]
    for l, wide in enumerate(widths):
        for r in range(2):
            kw[r, l, taps : taps + 1, :wide] = bias[0, r, :, l * LANES : l * LANES + wide]
    pl.semaphore_wait(barrier, len(greeted))

    def stage(source, dest):
        for l, wide in enumerate(widths):
            values = source[:, :, l * LANES : l * LANES + wide].astype(jnp.float32)
            dest[l, :, SUB : SUB + width, :wide] = values

    def shifted(ref, h, b):
        start = SUB - margin + b
        return ref[h, start : start + width, :]

    def conv(ref, r, l, flip, init):
        total = [init] * height
        for b in range(side):
            row = []
            for a in range(side):
                place = taps - 1 - (a * side + b) if flip else a * side + b
                row.append(jnp.broadcast_to(kw[r, l, place : place + 1, :], (width, LANES)))
            for source in range(height):
                values = shifted(ref, source, b)
                for a in range(side):
                    h = source - a + margin
                    if 0 <= h < height:
                        total[h] = total[h] + values * row[a]
        return total

    def rows(h):
        return pl.ds(h * width, width)

    def lane_tile(l):
        return pl.ds(pl.multiple_of(l * LANES, LANES), LANES)

    def link(t, c, dst):
        return pltpu.make_async_remote_copy(
            src_ref=tx.at[t, c],
            dst_ref=rx.at[t + 1, c],
            send_sem=send_sem.at[t, c],
            recv_sem=recv_sem.at[t + 1, c],
            device_id={"section": dst},
            device_id_type=MESH,
        )

    def inside(place):
        return jnp.logical_and(place >= 0, place < n)

    def arrive(t, c, src):
        remote = jnp.logical_and(t > 0, inside(src))

        @pl.when(remote)
        def _():
            pltpu.make_async_remote_copy(
                src_ref=tx.at[t, c],
                dst_ref=rx.at[t, c],
                send_sem=send_sem.at[t, c],
                recv_sem=recv_sem.at[t, c],
                device_id={"section": left},
                device_id_type=MESH,
            ).wait_recv()

        @pl.when(jnp.logical_not(remote))
        def _():
            pltpu.make_async_copy(act.at[0, 0, 0], rx.at[t, c], local_sem.at[t, c]).wait()

    def depart(t, c, dst):
        @pl.when(jnp.logical_and(t < ticks - 1, inside(dst)))
        def _():
            link(t, c, dst).start()

    def leave(c):
        target = (y_out if c < 2 else dx_out).at[c % 2, 0, 0]
        return pltpu.make_async_copy(tx.at[ticks - 1, c], target, out_sem.at[c])

    def forward(r, t):
        arrive(t, r, pos - 1 + 2 * r)
        stage(rx.at[t, r], xf)

        def tile(l, carry):
            first = jnp.broadcast_to(kw[r, l, taps : taps + 1, :], (width, LANES))
            total = conv(xf.at[l], r, l, False, first)
            for h in range(height):
                u = total[h]
                half = 0.5 * u
                th = jnp.tanh(u * (GELU_A + GELU_B * (u * u)))
                hid[rows(h), lane_tile(l)] = (half + half * th).astype(jnp.bfloat16)
            return carry

        lax.fori_loop(0, tiles, tile, 0)
        mixed = jnp.dot(hid[:, :chans], mix[r, :chans], preferred_element_type=jnp.float32)
        result = rx[t, r].astype(jnp.float32) + mixed.reshape(height, width, chans)
        tx[t, r] = result.astype(jnp.bfloat16)
        depart(t, r, pos + 1 - 2 * r)
        if t == ticks - 1:
            leave(r).start()

    def backward(r, t):
        pltpu.make_async_copy(stored_in.at[r, t], stored.at[r, t], stored_sem.at[r, t]).wait()
        stage(stored.at[r, t, 0, 0], xb.at[r, t])
        arrive(t, 2 + r, pos + 1 - 2 * r)

        def recompute(l, carry):
            incoming = rx[t, 2 + r].reshape(height * width, chans)
            hidden_grad[...] = lax.dot_general(
                incoming, mix[r, lane_tile(l)], (((1,), (1,)), ((), ())), preferred_element_type=jnp.float32
            )
            first = jnp.broadcast_to(kw[r, l, taps : taps + 1, :], (width, LANES))
            total = conv(xb.at[r, t, l], r, l, False, first)
            bias_sum = dk_acc[r, l, taps]
            for h in range(height):
                u = total[h]
                half = 0.5 * u
                square = u * u
                th = jnp.tanh(u * (GELU_A + GELU_B * square))
                hidb[r, t, rows(h), lane_tile(l)] = (half + half * th).astype(jnp.bfloat16)
                inner = GELU_A + (3.0 * GELU_B) * square
                slope = (0.5 + 0.5 * th) + half * (1.0 - th * th) * inner
                grad = hidden_grad[rows(h), :] * slope
                dpad[r, t, l, h, SUB : SUB + width, :] = grad
                for w in range(0, width, SUB):
                    bias_sum = bias_sum + grad[w : w + SUB]
            dk_acc[r, l, taps] = bias_sum
            return carry

        lax.fori_loop(0, tiles, recompute, 0)

        def spread(l, carry):
            total = conv(dpad.at[r, t, l], r, l, True, jnp.zeros((width, LANES), jnp.float32))
            for h in range(height):
                work[rows(h), lane_tile(l)] = total[h]
            return carry

        lax.fori_loop(0, tiles, spread, 0)
        result = rx[t, 2 + r].astype(jnp.float32) + work[:, :chans].reshape(height, width, chans)
        tx[t, 2 + r] = result.astype(jnp.bfloat16)
        depart(t, 2 + r, pos - 1 + 2 * r)
        if t == ticks - 1:
            leave(2 + r).start()

    def weights(r, t):
        def tile(l, carry):
            incoming = rx[t, 2 + r].reshape(height * width, chans)
            dp_acc[r, lane_tile(l), :] += lax.dot_general(
                hidb[r, t, :, lane_tile(l)], incoming, (((0,), (0,)), ((), ())), preferred_element_type=jnp.float32
            )
            grads = [dpad[r, t, l, h, SUB : SUB + width, :] for h in range(height)]
            for b in range(side):
                sums = [None] * side
                for source in range(height):
                    values = shifted(xb.at[r, t, l], source, b)
                    for a in range(side):
                        h = source - a + margin
                        if 0 <= h < height:
                            product = grads[h] * values
                            for w in range(0, width, SUB):
                                part = product[w : w + SUB]
                                sums[a] = part if sums[a] is None else sums[a] + part
                for a in range(side):
                    dk_acc[r, l, a * side + b] = dk_acc[r, l, a * side + b] + sums[a]
            return carry

        lax.fori_loop(0, tiles, tile, 0)

    def weights_of(r, start, stop):
        def one(t, carry):
            weights(r, t)
            return carry

        if stop > start:
            lax.fori_loop(start, stop, one, 0)

    def finish_small(r):
        for l, wide in enumerate(widths):
            total = jnp.sum(dk_acc[r, l], axis=1)
            small[r, : taps + 1, l * LANES : l * LANES + wide] = total[:, :wide]

    if share:
        swaps = [
            pltpu.make_async_remote_copy(
                src_ref=parcel.at[i],
                dst_ref=landed.at[i],
                send_sem=swap_send.at[i],
                recv_sem=swap_recv.at[i],
                device_id=mirror if i == 2 else peer,
                device_id_type=MESH,
            )
            for i in range(3)
        ]

    def mix_half(r, which):
        return dp_acc[r, pl.ds(pl.multiple_of(which * share, SUB), share), :]

    def small_half(r, which):
        return jnp.where(which == 0, small[r, :, :share], small[r, :, share:])

    def send_half(r):
        finish_small(r)
        parcel[r, :share, :] = mix_half(r, 1 - half).astype(jnp.bfloat16)
        parcel[r, share:, :share] = small_half(r, 1 - half).astype(jnp.bfloat16)
        swaps[r].start()

    def send_mirror():
        swaps[1].wait_recv()
        mixed = mix_half(1, half) + landed[1, :share, :].astype(jnp.float32)
        parcel[2, :share, :] = mixed.astype(jnp.bfloat16)
        rest = small_half(1, half) + landed[1, share:, :share].astype(jnp.float32)
        parcel[2, share:, :share] = rest.astype(jnp.bfloat16)
        swaps[2].start()

    last = ticks - 1
    for t in range(last):
        backward(1, t)
        if t == last - 1:
            weights_of(1, 0, last)
        backward(0, t)
        if t < last - 1:
            forward(0, t)
            forward(1, t)
    backward(1, last)
    weights_of(1, last, ticks)
    if share:
        send_half(1)
    if last:
        forward(0, last - 1)
        forward(1, last - 1)
    if share:
        send_mirror()
    backward(0, last)
    weights_of(0, 0, ticks)
    if share:
        send_half(0)
    forward(0, last)
    forward(1, last)

    for t in range(ticks - 1):
        for c, step in ((0, 1), (1, -1), (2, -1), (3, 1)):
            @pl.when(inside(pos + step))
            def _():
                link(t, c, pos + step).wait_send()
    if share:
        gm_out, gk_out, gb_out = outs[2:]
        swaps[0].wait_recv()
        swaps[2].wait_recv()
        mixed = mix_half(0, half) + landed[0, :share, :].astype(jnp.float32)
        gm_out[0, 0] = (mixed + landed[2, :share, :].astype(jnp.float32)) * factor
        rest = small_half(0, half) + landed[0, share:, :share].astype(jnp.float32)
        rest = (rest + landed[2, share:, :share].astype(jnp.float32)) * factor
        for a in range(side):
            for b in range(side):
                gk_out[0, a, b] = rest[a * side + b : a * side + b + 1]
        gb_out[0] = rest[taps : taps + 1]
        for swap in swaps:
            swap.wait_send()
    else:
        for r in range(2):
            finish_small(r)
        outs[2][...] = dp_acc[:, :chans]
        outs[3][...] = small[...]
    for c in range(4):
        leave(c).wait()


def place_kernel(*refs):
    half = len(refs) // 2
    sem = refs[-1]
    copies = []
    for source, dest in zip(refs[:half], refs[half:-1]):
        parts = [(source.at[r], dest.at[r]) for r in range(2)] if source.shape[0] == 2 else [(source, dest)]
        for one, other in parts:
            copies.append(pltpu.make_async_copy(one, other, sem.at[len(copies)]))
    for copy in copies:
        copy.start()
    for copy in copies:
        copy.wait()


def place(results):
    anywhere = pl.BlockSpec(memory_space=pl.ANY)
    return pl.pallas_call(
        place_kernel,
        out_shape=tuple(jax.ShapeDtypeStruct(x.shape, x.dtype) for x in results),
        in_specs=[anywhere] * len(results),
        out_specs=tuple(anywhere for _ in results),
        scratch_shapes=[pltpu.SemaphoreType.DMA((2 * len(results),))],
        compiler_params=pltpu.CompilerParams(vmem_limit_bytes=60 * 1024 * 1024),
        name="place",
    )(*results)


def relay(n, share, factor, act, cot, new_in, loss, stored, kern, bias, mix):
    ticks = stored.shape[1]
    height, width, chans = stored.shape[-3:]
    side = kern.shape[2]
    taps = side * side
    tiles = -(-chans // LANES)
    padded = tiles * LANES
    count = height * width
    across = width + 2 * SUB
    f32, bf16 = jnp.float32, jnp.bfloat16
    vmem = pl.BlockSpec(memory_space=pltpu.VMEM)
    anywhere = pl.BlockSpec(memory_space=pl.ANY)
    small = -(-(taps + 1) // 16) * 16
    if share:
        sums = [(1, 1, share, chans), (1, side, side, 1, share), (1, 1, share)]
    else:
        sums = [(2, chans, chans), (2, small, chans)]
    return pl.pallas_call(
        functools.partial(relay_kernel, n, share, factor),
        out_shape=(
            jax.ShapeDtypeStruct(act.shape, bf16),
            jax.ShapeDtypeStruct(cot.shape, bf16),
            *(jax.ShapeDtypeStruct(shape, f32) for shape in sums),
        ),
        in_specs=[anywhere] * 8,
        out_specs=(anywhere, anywhere, *(vmem for _ in sums)),
        scratch_shapes=[
            pltpu.VMEM((tiles, height, across, LANES), f32),
            pltpu.VMEM((2, ticks, tiles, height, across, LANES), f32),
            pltpu.VMEM((2, ticks, tiles, height, across, LANES), f32),
            pltpu.VMEM((count, padded), bf16),
            pltpu.VMEM((2, ticks, count, padded), bf16),
            pltpu.VMEM((count, LANES), f32),
            pltpu.VMEM((count, padded), f32),
            pltpu.VMEM((2, tiles, small, LANES), f32),
            pltpu.VMEM((2, tiles, taps + 1, SUB, LANES), f32),
            pltpu.VMEM((2, padded, chans), f32),
            pltpu.VMEM((2, small, chans), f32),
            pltpu.VMEM((ticks, 4, height, width, chans), bf16),
            pltpu.VMEM((ticks, 4, height, width, chans), bf16),
            pltpu.VMEM(stored.shape, bf16),
            pltpu.VMEM(kern.shape, bf16),
            pltpu.VMEM(bias.shape, f32),
            pltpu.VMEM((2, padded, chans), bf16),
            pltpu.VMEM((3, share + small, chans), bf16),
            pltpu.VMEM((3, share + small, chans), bf16),
            pltpu.SemaphoreType.DMA((ticks, 4)),
            pltpu.SemaphoreType.DMA((ticks, 4)),
            pltpu.SemaphoreType.DMA((ticks, 4)),
            pltpu.SemaphoreType.DMA((4,)),
            pltpu.SemaphoreType.DMA((3,)),
            pltpu.SemaphoreType.DMA((2, ticks)),
            pltpu.SemaphoreType.DMA((3,)),
            pltpu.SemaphoreType.DMA((3,)),
        ],
        compiler_params=pltpu.CompilerParams(
            collective_id=0, has_side_effects=True, vmem_limit_bytes=60 * 1024 * 1024
        ),
        name="relay",
    )(act, cot, new_in, loss, stored, kern, bias, mix)


def per_device(
    activations, stored_inputs, cotangents, new_inputs, loss_grad, depth_kernel, depth_bias, mixing
):
    sections = lax.axis_size("section")
    copies = lax.axis_size("dp")
    side = depth_kernel.shape[-2]
    taps = side * side
    ticks = stored_inputs.shape[1]
    chans = mixing.shape[-1]
    map_rows = activations.shape[3] * activations.shape[4]
    factor = (2.0 * ticks * activations.shape[2] * copies * map_rows) ** (-0.5)
    in_kernel = copies == 2 and sections % 2 == 0 and chans % 32 == 0
    share = chans // 2 if in_kernel else 0
    outputs, grads, *sums = relay(
        sections, share, factor, activations, cotangents, new_inputs, loss_grad,
        stored_inputs, depth_kernel.transpose(0, 2, 3, 4, 1, 5), depth_bias, mixing,
    )
    if in_kernel:
        outputs, grads, grad_mixing, grad_kernel, grad_bias = place((outputs, grads, *sums))
        return (outputs, grads, grad_kernel.transpose(0, 3, 1, 2, 4), grad_bias, grad_mixing)
    mix_share = lax.psum_scatter(sums[0], "dp", scatter_dimension=1, tiled=True)
    small_share = lax.psum_scatter(sums[1], "dp", scatter_dimension=2, tiled=True)
    swap = [(i, sections - 1 - i) for i in range(sections)]
    mix_other, small_other = lax.ppermute((mix_share[1], small_share[1]), "section", swap)
    grad_mixing = ((mix_share[0] + mix_other) * factor)[None, None]
    small = (small_share[0] + small_other) * factor
    grad_kernel = small[:taps].reshape(1, 1, side, side, -1)
    grad_bias = small[taps][None, None]
    return (outputs, grads, grad_kernel, grad_bias, grad_mixing)


def solution(mesh):
    return jax.shard_map(
        per_device,
        mesh=mesh,
        in_specs=(
            P(None, "section", "dp", None, None, None),
            P(None, None, "section", "dp", None, None, None),
            P(None, "section", "dp", None, None, None),
            P(None, None, "dp", None, None, None),
            P(None, None, "dp", None, None, None),
            P("section", None, None, None, None, None),
            P("section", None, None, None),
            P("section", None, None, None, None),
        ),
        out_specs=(
            P(None, "section", "dp", None, None, None),
            P(None, "section", "dp", None, None, None),
            P("section", None, None, None, "dp"),
            P("section", None, "dp"),
            P("section", None, "dp", None),
        ),
        check_vma=False,
    )
```

```python
import functools
import math

import jax
import jax.numpy as jnp
from jax import lax
from jax.experimental import pallas as pl
from jax.experimental.pallas import tpu as pltpu
from jax.sharding import PartitionSpec as P

LANES = 128
SUB = 8
GELU_A = math.sqrt(2.0 / math.pi)
GELU_B = GELU_A * 0.044715
MESH = pl.DeviceIdType.MESH


def relay_kernel(
    n, share, factor, act, cot, new_in, loss, stored_in, kern_in, bias_in, mix_in, *refs
):
    outs, refs = refs[:4 + (share > 0)], refs[4 + (share > 0):]
    y_out, dx_out = outs[:2]
    (
        xf, xb, dpad, hid, hidb, hidden_grad, work, kw, dk_acc, dp_acc, small, rx, tx, mail_in, mail_out,
        stored, kern, bias, mix, parcel, landed,
        local_sem, send_sem, recv_sem, out_sem, load_sem, stored_sem, swap_send, swap_recv,
    ) = refs
    ticks = stored.shape[1]
    height, width, chans = stored.shape[-3:]
    side = kern.shape[2]
    margin = side // 2
    tiles = xf.shape[0]
    taps = side * side
    widths = [min(LANES, chans - t * LANES) for t in range(tiles)]
    pos = lax.axis_index("section")
    right, left = lax.rem(pos + 1, n), lax.rem(pos + n - 1, n)

    loads = [
        pltpu.make_async_copy(source, dest, load_sem.at[i])
        for i, (source, dest) in enumerate(
            ((kern_in, kern), (bias_in, bias), (mix_in.at[0, :, 0], mix.at[:, :chans]))
        )
    ]
    for load in loads:
        load.start()
    pltpu.make_async_copy(stored_in.at[1, 0], stored.at[1, 0], stored_sem.at[1, 0]).start()
    for c in range(4):
        first = (act if c < 2 else cot).at[c % 2, 0, 0]
        pltpu.make_async_copy(first, rx.at[0, c], local_sem.at[0, c]).start()
    for t in range(ticks):
        for r in (1, 0):
            if (r, t) != (1, 0):
                pltpu.make_async_copy(stored_in.at[r, t], stored.at[r, t], stored_sem.at[r, t]).start()
    for c, entry in ((0, 0), (1, n - 1), (2, n - 1), (3, 0)):
        @pl.when(pos == entry)
        def _():
            for t in range(1, ticks):
                source = (new_in if c < 2 else loss).at[c % 2, t - 1, 0]
                pltpu.make_async_copy(source, rx.at[t, c], local_sem.at[t, c]).start()

    barrier = pltpu.get_barrier_semaphore()
    greeted = [{"section": left}, {"section": right}]
    if share:
        half = lax.axis_index("dp")
        peer, mirror = {"dp": 1 - half}, {"section": n - 1 - pos}
        greeted += [peer, mirror]
    for other in greeted:
        pl.semaphore_signal(barrier, inc=1, device_id=other, device_id_type=MESH)

    for ref in (xf, xb, dpad):
        edge = jnp.zeros(ref.shape[:-2] + (SUB, LANES), jnp.float32)
        ref[..., :SUB, :] = edge
        ref[..., SUB + width :, :] = edge
    dk_acc[...] = jnp.zeros(dk_acc.shape, jnp.float32)
    dp_acc[...] = jnp.zeros(dp_acc.shape, jnp.float32)
    small[...] = jnp.zeros(small.shape, jnp.float32)
    for load in loads:
        load.wait()
    for a in range(side):
        for b in range(side):
            pair = kern[0, 0, a, b].astype(jnp.float32)
            place = a * side + b
            for l, wide in enumerate(widths):
                for r in range(2):
                    kw[r, l, place : place + 1, :wide] = pair[r : r + 1, l * LANES : l * LANES + wide]
    for l, wide in enumerate(widths):
        for r in range(2):
            kw[r, l, taps : taps + 1, :wide] = bias[0, r, :, l * LANES : l * LANES + wide]
    pl.semaphore_wait(barrier, len(greeted))

    def stage(source, dest):
        for l, wide in enumerate(widths):
            values = source[:, :, l * LANES : l * LANES + wide].astype(jnp.float32)
            dest[l, :, SUB : SUB + width, :wide] = values

    def shifted(ref, h, b):
        start = SUB - margin + b
        return ref[h, start : start + width, :]

    def conv(ref, r, l, flip, init):
        total = [init] * height
        for b in range(side):
            row = []
            for a in range(side):
                place = taps - 1 - (a * side + b) if flip else a * side + b
                row.append(jnp.broadcast_to(kw[r, l, place : place + 1, :], (width, LANES)))
            for source in range(height):
                values = shifted(ref, source, b)
                for a in range(side):
                    h = source - a + margin
                    if 0 <= h < height:
                        total[h] = total[h] + values * row[a]
        return total

    def rows(h):
        return pl.ds(h * width, width)

    def lane_tile(l):
        return pl.ds(pl.multiple_of(l * LANES, LANES), LANES)

    def link(t, c, dst):
        return pltpu.make_async_remote_copy(
            src_ref=mail_out.at[t, c],
            dst_ref=mail_in.at[t, c],
            send_sem=send_sem.at[t, c],
            recv_sem=recv_sem.at[t + 1, c],
            device_id={"section": dst},
            device_id_type=MESH,
        )

    def inside(place):
        return jnp.logical_and(place >= 0, place < n)

    whole, rest = divmod(chans, LANES)
    count = height * width
    groups = fold_groups(chans, height)
    group_rows = count // groups

    def pack(c, t):
        for l in range(whole):
            mail_out[t, c, l * count : (l + 1) * count, :] = tx[
                t, c, :, :, l * LANES : (l + 1) * LANES
            ].reshape(count, LANES)
        if rest:
            ends = tx[t, c, :, :, whole * LANES :].reshape(count, rest).astype(jnp.float32)
            parts = [ends[g * group_rows : (g + 1) * group_rows] for g in range(groups)]
            folded = jnp.concatenate(parts, axis=1).astype(jnp.bfloat16)
            mail_out[t, c, whole * count :, : groups * rest] = folded

    def unpack(c, t):
        for l in range(whole):
            rx[t, c, :, :, l * LANES : (l + 1) * LANES] = mail_in[
                t - 1, c, l * count : (l + 1) * count, :
            ].reshape(height, width, LANES)
        if rest:
            folded = mail_in[t - 1, c, whole * count :, :].astype(jnp.float32)
            for g in range(groups):
                part = folded[:, g * rest : (g + 1) * rest].astype(jnp.bfloat16)
                rx[t, c, g * height // groups : (g + 1) * height // groups, :, whole * LANES :] = part.reshape(
                    height // groups, width, rest
                )

    def arrive(t, c, src):
        def local():
            pltpu.make_async_copy(act.at[0, 0, 0], rx.at[t, c], local_sem.at[t, c]).wait()

        if t == 0:
            local()
            return

        @pl.when(inside(src))
        def _():
            pltpu.make_async_remote_copy(
                src_ref=mail_out.at[t - 1, c],
                dst_ref=mail_in.at[t - 1, c],
                send_sem=send_sem.at[t - 1, c],
                recv_sem=recv_sem.at[t, c],
                device_id={"section": left},
                device_id_type=MESH,
            ).wait_recv()
            unpack(c, t)

        @pl.when(jnp.logical_not(inside(src)))
        def _():
            local()

    def depart(t, c, dst):
        if t == ticks - 1:
            return

        @pl.when(inside(dst))
        def _():
            pack(c, t)
            link(t, c, dst).start()

    def leave(c):
        target = (y_out if c < 2 else dx_out).at[c % 2, 0, 0]
        return pltpu.make_async_copy(tx.at[ticks - 1, c], target, out_sem.at[c])

    def forward(r, t):
        arrive(t, r, pos - 1 + 2 * r)
        stage(rx.at[t, r], xf)

        def tile(l, carry):
            first = jnp.broadcast_to(kw[r, l, taps : taps + 1, :], (width, LANES))
            total = conv(xf.at[l], r, l, False, first)
            for h in range(height):
                u = total[h]
                half = 0.5 * u
                th = jnp.tanh(u * (GELU_A + GELU_B * (u * u)))
                hid[rows(h), lane_tile(l)] = (half + half * th).astype(jnp.bfloat16)
            return carry

        lax.fori_loop(0, tiles, tile, 0)
        mixed = jnp.dot(hid[:, :chans], mix[r, :chans], preferred_element_type=jnp.float32)
        result = rx[t, r].astype(jnp.float32) + mixed.reshape(height, width, chans)
        tx[t, r] = result.astype(jnp.bfloat16)
        depart(t, r, pos + 1 - 2 * r)
        if t == ticks - 1:
            leave(r).start()

    def backward(r, t):
        pltpu.make_async_copy(stored_in.at[r, t], stored.at[r, t], stored_sem.at[r, t]).wait()
        stage(stored.at[r, t, 0, 0], xb.at[r, t])
        arrive(t, 2 + r, pos + 1 - 2 * r)

        def recompute(l, carry):
            incoming = rx[t, 2 + r].reshape(height * width, chans)
            hidden_grad[...] = lax.dot_general(
                incoming, mix[r, lane_tile(l)], (((1,), (1,)), ((), ())), preferred_element_type=jnp.float32
            )
            first = jnp.broadcast_to(kw[r, l, taps : taps + 1, :], (width, LANES))
            total = conv(xb.at[r, t, l], r, l, False, first)
            bias_sum = dk_acc[r, l, taps]
            for h in range(height):
                u = total[h]
                half = 0.5 * u
                square = u * u
                th = jnp.tanh(u * (GELU_A + GELU_B * square))
                hidb[r, t, rows(h), lane_tile(l)] = (half + half * th).astype(jnp.bfloat16)
                inner = GELU_A + (3.0 * GELU_B) * square
                slope = (0.5 + 0.5 * th) + half * (1.0 - th * th) * inner
                grad = hidden_grad[rows(h), :] * slope
                dpad[r, t, l, h, SUB : SUB + width, :] = grad
                for w in range(0, width, SUB):
                    bias_sum = bias_sum + grad[w : w + SUB]
            dk_acc[r, l, taps] = bias_sum
            return carry

        lax.fori_loop(0, tiles, recompute, 0)

        def spread(l, carry):
            total = conv(dpad.at[r, t, l], r, l, True, jnp.zeros((width, LANES), jnp.float32))
            for h in range(height):
                work[rows(h), lane_tile(l)] = total[h]
            return carry

        lax.fori_loop(0, tiles, spread, 0)
        result = rx[t, 2 + r].astype(jnp.float32) + work[:, :chans].reshape(height, width, chans)
        tx[t, 2 + r] = result.astype(jnp.bfloat16)
        depart(t, 2 + r, pos - 1 + 2 * r)
        if t == ticks - 1:
            leave(2 + r).start()

    def weights(r, t):
        def tile(l, carry):
            incoming = rx[t, 2 + r].reshape(height * width, chans)
            dp_acc[r, lane_tile(l), :] += lax.dot_general(
                hidb[r, t, :, lane_tile(l)], incoming, (((0,), (0,)), ((), ())), preferred_element_type=jnp.float32
            )
            grads = [dpad[r, t, l, h, SUB : SUB + width, :] for h in range(height)]
            for b in range(side):
                sums = [None] * side
                for source in range(height):
                    values = shifted(xb.at[r, t, l], source, b)
                    for a in range(side):
                        h = source - a + margin
                        if 0 <= h < height:
                            product = grads[h] * values
                            for w in range(0, width, SUB):
                                part = product[w : w + SUB]
                                sums[a] = part if sums[a] is None else sums[a] + part
                for a in range(side):
                    dk_acc[r, l, a * side + b] = dk_acc[r, l, a * side + b] + sums[a]
            return carry

        lax.fori_loop(0, tiles, tile, 0)

    def weights_of(r, start, stop):
        def one(t, carry):
            weights(r, t)
            return carry

        if stop > start:
            lax.fori_loop(start, stop, one, 0)

    def finish_small(r):
        for l, wide in enumerate(widths):
            total = jnp.sum(dk_acc[r, l], axis=1)
            small[r, : taps + 1, l * LANES : l * LANES + wide] = total[:, :wide]

    if share:
        swaps = [
            pltpu.make_async_remote_copy(
                src_ref=parcel.at[i],
                dst_ref=landed.at[i],
                send_sem=swap_send.at[i],
                recv_sem=swap_recv.at[i],
                device_id=mirror if i == 2 else peer,
                device_id_type=MESH,
            )
            for i in range(3)
        ]

    def mix_half(r, which):
        return dp_acc[r, pl.ds(pl.multiple_of(which * share, SUB), share), :]

    def small_half(r, which):
        return jnp.where(which == 0, small[r, :, :share], small[r, :, share:])

    share_whole = chans // LANES
    rest_rows = parcel_rest_rows(share, chans)
    bulk = share_whole * share
    small_rows = small.shape[1]

    def fill(i, mixed, ends):
        for l in range(share_whole):
            parcel[i, l * share : (l + 1) * share, :] = mixed[:, l * LANES : (l + 1) * LANES].astype(jnp.bfloat16)
        if rest_rows:
            for g in range(-(-share // rest_rows)):
                part = mixed[g * rest_rows : (g + 1) * rest_rows, share_whole * LANES :]
                parcel[i, bulk : bulk + part.shape[0], g * rest : (g + 1) * rest] = part.astype(jnp.bfloat16)
        for l in range(-(-share // LANES)):
            part = ends[:, l * LANES : (l + 1) * LANES]
            start = bulk + rest_rows + l * small_rows
            parcel[i, start : start + small_rows, : part.shape[1]] = part.astype(jnp.bfloat16)
        swaps[i].start()

    def opened(i):
        mixed = [landed[i, l * share : (l + 1) * share, :] for l in range(share_whole)]
        if rest_rows:
            parts = []
            for g in range(-(-share // rest_rows)):
                wanted = min(rest_rows, share - g * rest_rows)
                parts.append(landed[i, bulk : bulk + wanted, :].astype(jnp.float32)[:, g * rest : (g + 1) * rest])
            mixed.append(jnp.concatenate(parts, axis=0))
        ends = []
        for l in range(-(-share // LANES)):
            start = bulk + rest_rows + l * small_rows
            ends.append(landed[i, start : start + small_rows, : min(LANES, share - l * LANES)])
        return tuple(
            jnp.concatenate([x.astype(jnp.float32) for x in parts], axis=1) for parts in (mixed, ends)
        )

    def send_half(r):
        finish_small(r)
        fill(r, mix_half(r, 1 - half), small_half(r, 1 - half))

    def send_mirror():
        swaps[1].wait_recv()
        mixed, ends = opened(1)
        fill(2, mix_half(1, half) + mixed, small_half(1, half) + ends)

    last = ticks - 1
    for t in range(last):
        backward(1, t)
        forward(0, t)
        forward(1, t)
        if t:
            weights(1, t - 1)
        backward(0, t)
    if last:
        weights(1, last - 1)
    backward(1, last)
    weights(1, last)
    if share:
        send_half(1)
    weights_of(0, 0, min(1, last))
    if share:
        send_mirror()
    weights_of(0, min(1, last), last)
    backward(0, last)
    weights(0, last)
    if share:
        send_half(0)
    forward(0, last)
    forward(1, last)

    for t in range(ticks - 1):
        for c, step in ((0, 1), (1, -1), (2, -1), (3, 1)):
            @pl.when(inside(pos + step))
            def _():
                link(t, c, pos + step).wait_send()
    if share:
        gm_out, gk_out, gb_out = outs[2:]
        swaps[0].wait_recv()
        swaps[2].wait_recv()
        near, far = opened(0), opened(2)
        gm_out[0, 0] = (mix_half(0, half) + near[0] + far[0]) * factor
        ends = (small_half(0, half) + near[1] + far[1]) * factor
        for a in range(side):
            for b in range(side):
                gk_out[0, a, b] = ends[a * side + b : a * side + b + 1]
        gb_out[0] = ends[taps : taps + 1]
        for swap in swaps:
            swap.wait_send()
    else:
        for r in range(2):
            finish_small(r)
        outs[2][...] = dp_acc[:, :chans]
        outs[3][...] = small[...]
    for c in range(4):
        leave(c).wait()


def place_kernel(*refs):
    half = len(refs) // 3
    sources, targets, held = refs[:half], refs[half : 2 * half], refs[2 * half : 3 * half]
    in_sem, out_sem = refs[3 * half :]
    trips = []
    for trio in zip(sources, held, targets):
        for source, stop, target in [[x.at[r] for x in trio] for r in range(2)] if trio[0].shape[0] == 2 else [trio]:
            i = len(trips)
            trips.append(
                (
                    pltpu.make_async_copy(source, stop, in_sem.at[i]),
                    pltpu.make_async_copy(stop, target, out_sem.at[i]),
                )
            )
    for fetch, _ in trips:
        fetch.start()
    for fetch, put in trips:
        fetch.wait()
        put.start()
    for _, put in trips:
        put.wait()


def place(results):
    anywhere = pl.BlockSpec(memory_space=pl.ANY)
    return pl.pallas_call(
        place_kernel,
        out_shape=tuple(jax.ShapeDtypeStruct(x.shape, x.dtype) for x in results),
        in_specs=[anywhere] * len(results),
        out_specs=tuple(anywhere for _ in results),
        scratch_shapes=[
            *(pltpu.VMEM(x.shape, x.dtype) for x in results),
            pltpu.SemaphoreType.DMA((2 * len(results),)),
            pltpu.SemaphoreType.DMA((2 * len(results),)),
        ],
        compiler_params=pltpu.CompilerParams(vmem_limit_bytes=60 * 1024 * 1024),
        name="place",
    )(*results)


def fold_groups(chans, height):
    rest = chans % LANES
    groups = LANES // rest if rest else 1
    return groups if height % groups == 0 else 1


def parcel_rest_rows(share, chans):
    rest = chans % LANES
    if not rest:
        return 0
    return -(-share // (LANES // rest * 16)) * 16


def relay(n, share, factor, act, cot, new_in, loss, stored, kern, bias, mix):
    ticks = stored.shape[1]
    height, width, chans = stored.shape[-3:]
    side = kern.shape[2]
    taps = side * side
    tiles = -(-chans // LANES)
    padded = tiles * LANES
    count = height * width
    across = width + 2 * SUB
    f32, bf16 = jnp.float32, jnp.bfloat16
    vmem = pl.BlockSpec(memory_space=pltpu.VMEM)
    anywhere = pl.BlockSpec(memory_space=pl.ANY)
    small = -(-(taps + 1) // 16) * 16
    mail = chans // LANES * count
    if chans % LANES:
        mail += count // fold_groups(chans, height)
    parcel = chans // LANES * share + parcel_rest_rows(share, chans) + -(-share // LANES) * small
    if share:
        sums = [(1, 1, share, chans), (1, side, side, 1, share), (1, 1, share)]
    else:
        sums = [(2, chans, chans), (2, small, chans)]
    return pl.pallas_call(
        functools.partial(relay_kernel, n, share, factor),
        out_shape=(
            jax.ShapeDtypeStruct(act.shape, bf16),
            jax.ShapeDtypeStruct(cot.shape, bf16),
            *(jax.ShapeDtypeStruct(shape, f32) for shape in sums),
        ),
        in_specs=[anywhere] * 8,
        out_specs=(anywhere, anywhere, *(vmem for _ in sums)),
        scratch_shapes=[
            pltpu.VMEM((tiles, height, across, LANES), f32),
            pltpu.VMEM((2, ticks, tiles, height, across, LANES), f32),
            pltpu.VMEM((2, ticks, tiles, height, across, LANES), f32),
            pltpu.VMEM((count, padded), bf16),
            pltpu.VMEM((2, ticks, count, padded), bf16),
            pltpu.VMEM((count, LANES), f32),
            pltpu.VMEM((count, padded), f32),
            pltpu.VMEM((2, tiles, small, LANES), f32),
            pltpu.VMEM((2, tiles, taps + 1, SUB, LANES), f32),
            pltpu.VMEM((2, padded, chans), f32),
            pltpu.VMEM((2, small, chans), f32),
            pltpu.VMEM((ticks, 4, height, width, chans), bf16),
            pltpu.VMEM((ticks, 4, height, width, chans), bf16),
            pltpu.VMEM((max(ticks - 1, 1), 4, mail, LANES), bf16),
            pltpu.VMEM((max(ticks - 1, 1), 4, mail, LANES), bf16),
            pltpu.VMEM(stored.shape, bf16),
            pltpu.VMEM(kern.shape, bf16),
            pltpu.VMEM(bias.shape, f32),
            pltpu.VMEM((2, padded, chans), bf16),
            pltpu.VMEM((3, parcel, LANES), bf16),
            pltpu.VMEM((3, parcel, LANES), bf16),
            pltpu.SemaphoreType.DMA((ticks, 4)),
            pltpu.SemaphoreType.DMA((ticks, 4)),
            pltpu.SemaphoreType.DMA((ticks, 4)),
            pltpu.SemaphoreType.DMA((4,)),
            pltpu.SemaphoreType.DMA((3,)),
            pltpu.SemaphoreType.DMA((2, ticks)),
            pltpu.SemaphoreType.DMA((3,)),
            pltpu.SemaphoreType.DMA((3,)),
        ],
        compiler_params=pltpu.CompilerParams(
            collective_id=0, has_side_effects=True, vmem_limit_bytes=60 * 1024 * 1024
        ),
        name="relay",
    )(act, cot, new_in, loss, stored, kern, bias, mix)


def per_device(
    activations, stored_inputs, cotangents, new_inputs, loss_grad, depth_kernel, depth_bias, mixing
):
    sections = lax.axis_size("section")
    copies = lax.axis_size("dp")
    side = depth_kernel.shape[-2]
    taps = side * side
    ticks = stored_inputs.shape[1]
    chans = mixing.shape[-1]
    map_rows = activations.shape[3] * activations.shape[4]
    factor = (2.0 * ticks * activations.shape[2] * copies * map_rows) ** (-0.5)
    in_kernel = copies == 2 and sections % 2 == 0 and chans % 32 == 0
    share = chans // 2 if in_kernel else 0
    outputs, grads, *sums = relay(
        sections, share, factor, activations, cotangents, new_inputs, loss_grad,
        stored_inputs, depth_kernel.transpose(0, 2, 3, 4, 1, 5), depth_bias, mixing,
    )
    if in_kernel:
        outputs, grads, grad_mixing, grad_kernel, grad_bias = place((outputs, grads, *sums))
        return (outputs, grads, grad_kernel.transpose(0, 3, 1, 2, 4), grad_bias, grad_mixing)
    mix_share = lax.psum_scatter(sums[0], "dp", scatter_dimension=1, tiled=True)
    small_share = lax.psum_scatter(sums[1], "dp", scatter_dimension=2, tiled=True)
    swap = [(i, sections - 1 - i) for i in range(sections)]
    mix_other, small_other = lax.ppermute((mix_share[1], small_share[1]), "section", swap)
    grad_mixing = ((mix_share[0] + mix_other) * factor)[None, None]
    small = (small_share[0] + small_other) * factor
    grad_kernel = small[:taps].reshape(1, 1, side, side, -1)
    grad_bias = small[taps][None, None]
    return (outputs, grads, grad_kernel, grad_bias, grad_mixing)


def solution(mesh):
    return jax.shard_map(
        per_device,
        mesh=mesh,
        in_specs=(
            P(None, "section", "dp", None, None, None),
            P(None, None, "section", "dp", None, None, None),
            P(None, "section", "dp", None, None, None),
            P(None, None, "dp", None, None, None),
            P(None, None, "dp", None, None, None),
            P("section", None, None, None, None, None),
            P("section", None, None, None),
            P("section", None, None, None, None),
        ),
        out_specs=(
            P(None, "section", "dp", None, None, None),
            P(None, "section", "dp", None, None, None),
            P("section", None, None, None, "dp"),
            P("section", None, "dp"),
            P("section", None, "dp", None),
        ),
        check_vma=False,
    )
```

```python
import functools
import math

import jax
import jax.numpy as jnp
from jax import lax
from jax.experimental import pallas as pl
from jax.experimental.pallas import tpu as pltpu
from jax.sharding import PartitionSpec as P

LANES = 128
SUB = 8
GELU_A = math.sqrt(2.0 / math.pi)
GELU_B = GELU_A * 0.044715
MESH = pl.DeviceIdType.MESH


def relay_kernel(
    n, share, factor, act, cot, new_in, loss, stored_in, kern_in, bias_in, mix_in, *refs
):
    outs, refs = refs[:4 + (share > 0)], refs[4 + (share > 0):]
    y_out, dx_out = outs[:2]
    (
        xf, xb, dpad, hid, hidb, hidden_grad, work, kw, dk_acc, dp_acc, small, rx, tx, mail_in, mail_out,
        stored, kern, bias, mix, parcel, landed,
        local_sem, send_sem, recv_sem, out_sem, load_sem, stored_sem, swap_send, swap_recv,
    ) = refs
    ticks = stored.shape[1]
    height, width, chans = stored.shape[-3:]
    side = kern.shape[2]
    margin = side // 2
    tiles = xf.shape[0]
    taps = side * side
    widths = [min(LANES, chans - t * LANES) for t in range(tiles)]
    pos = lax.axis_index("section")
    right, left = lax.rem(pos + 1, n), lax.rem(pos + n - 1, n)

    loads = [
        pltpu.make_async_copy(source, dest, load_sem.at[i])
        for i, (source, dest) in enumerate(
            ((kern_in, kern), (bias_in, bias), (mix_in.at[0, :, 0], mix.at[:, :chans]))
        )
    ]
    for load in loads:
        load.start()
    pltpu.make_async_copy(stored_in.at[1, 0], stored.at[1, 0], stored_sem.at[1, 0]).start()
    for c in range(4):
        first = (act if c < 2 else cot).at[c % 2, 0, 0]
        pltpu.make_async_copy(first, rx.at[0, c], local_sem.at[0, c]).start()
    for t in range(ticks):
        for r in (1, 0):
            if (r, t) != (1, 0):
                pltpu.make_async_copy(stored_in.at[r, t], stored.at[r, t], stored_sem.at[r, t]).start()
    for c, entry in ((0, 0), (1, n - 1), (2, n - 1), (3, 0)):
        @pl.when(pos == entry)
        def _():
            for t in range(1, ticks):
                source = (new_in if c < 2 else loss).at[c % 2, t - 1, 0]
                pltpu.make_async_copy(source, rx.at[t, c], local_sem.at[t, c]).start()

    barrier = pltpu.get_barrier_semaphore()
    greeted = [{"section": left}, {"section": right}]
    if share:
        half = lax.axis_index("dp")
        peer, mirror = {"dp": 1 - half}, {"section": n - 1 - pos}
        greeted += [peer, mirror]
    for other in greeted:
        pl.semaphore_signal(barrier, inc=1, device_id=other, device_id_type=MESH)

    for ref in (xf, xb, dpad):
        edge = jnp.zeros(ref.shape[:-2] + (SUB, LANES), jnp.float32)
        ref[..., :SUB, :] = edge
        ref[..., SUB + width :, :] = edge
    dk_acc[...] = jnp.zeros(dk_acc.shape, jnp.float32)
    dp_acc[...] = jnp.zeros(dp_acc.shape, jnp.float32)
    small[...] = jnp.zeros(small.shape, jnp.float32)
    for load in loads:
        load.wait()
    for a in range(side):
        for b in range(side):
            pair = kern[0, 0, a, b].astype(jnp.float32)
            place = a * side + b
            for l, wide in enumerate(widths):
                for r in range(2):
                    kw[r, l, place : place + 1, :wide] = pair[r : r + 1, l * LANES : l * LANES + wide]
    for l, wide in enumerate(widths):
        for r in range(2):
            kw[r, l, taps : taps + 1, :wide] = bias[0, r, :, l * LANES : l * LANES + wide]

    def stage(source, dest):
        for l, wide in enumerate(widths):
            values = source[:, :, l * LANES : l * LANES + wide].astype(jnp.float32)
            dest[l, :, SUB : SUB + width, :wide] = values

    def shifted(ref, h, b):
        start = SUB - margin + b
        return ref[h, start : start + width, :]

    def conv(ref, r, l, flip, init):
        total = [init] * height
        for b in range(side):
            row = []
            for a in range(side):
                place = taps - 1 - (a * side + b) if flip else a * side + b
                row.append(jnp.broadcast_to(kw[r, l, place : place + 1, :], (width, LANES)))
            for source in range(height):
                values = shifted(ref, source, b)
                for a in range(side):
                    h = source - a + margin
                    if 0 <= h < height:
                        total[h] = total[h] + values * row[a]
        return total

    def rows(h):
        return pl.ds(h * width, width)

    def lane_tile(l):
        return pl.ds(pl.multiple_of(l * LANES, LANES), LANES)

    def link(t, c, dst):
        return pltpu.make_async_remote_copy(
            src_ref=mail_out.at[t, c],
            dst_ref=mail_in.at[t, c],
            send_sem=send_sem.at[t, c],
            recv_sem=recv_sem.at[t + 1, c],
            device_id={"section": dst},
            device_id_type=MESH,
        )

    def inside(place):
        return jnp.logical_and(place >= 0, place < n)

    whole, rest = divmod(chans, LANES)
    count = height * width
    groups = fold_groups(chans, height)
    group_rows = count // groups

    def pack(c, t):
        for l in range(whole):
            mail_out[t, c, l * count : (l + 1) * count, :] = tx[
                t, c, :, :, l * LANES : (l + 1) * LANES
            ].reshape(count, LANES)
        if rest:
            ends = tx[t, c, :, :, whole * LANES :].reshape(count, rest).astype(jnp.float32)
            parts = [ends[g * group_rows : (g + 1) * group_rows] for g in range(groups)]
            folded = jnp.concatenate(parts, axis=1).astype(jnp.bfloat16)
            mail_out[t, c, whole * count :, : groups * rest] = folded

    def unpack(c, t):
        for l in range(whole):
            rx[t, c, :, :, l * LANES : (l + 1) * LANES] = mail_in[
                t - 1, c, l * count : (l + 1) * count, :
            ].reshape(height, width, LANES)
        if rest:
            folded = mail_in[t - 1, c, whole * count :, :].astype(jnp.float32)
            for g in range(groups):
                part = folded[:, g * rest : (g + 1) * rest].astype(jnp.bfloat16)
                rx[t, c, g * height // groups : (g + 1) * height // groups, :, whole * LANES :] = part.reshape(
                    height // groups, width, rest
                )

    def arrive(t, c, src):
        def local():
            pltpu.make_async_copy(act.at[0, 0, 0], rx.at[t, c], local_sem.at[t, c]).wait()

        if t == 0:
            local()
            return

        @pl.when(inside(src))
        def _():
            pltpu.make_async_remote_copy(
                src_ref=mail_out.at[t - 1, c],
                dst_ref=mail_in.at[t - 1, c],
                send_sem=send_sem.at[t - 1, c],
                recv_sem=recv_sem.at[t, c],
                device_id={"section": left},
                device_id_type=MESH,
            ).wait_recv()
            unpack(c, t)

        @pl.when(jnp.logical_not(inside(src)))
        def _():
            local()

    def depart(t, c, dst):
        if t == ticks - 1:
            return

        @pl.when(inside(dst))
        def _():
            pack(c, t)
            link(t, c, dst).start()

    def leave(c):
        target = (y_out if c < 2 else dx_out).at[c % 2, 0, 0]
        return pltpu.make_async_copy(tx.at[ticks - 1, c], target, out_sem.at[c])

    def forward(r, t):
        arrive(t, r, pos - 1 + 2 * r)
        stage(rx.at[t, r], xf)

        def tile(l, carry):
            first = jnp.broadcast_to(kw[r, l, taps : taps + 1, :], (width, LANES))
            total = conv(xf.at[l], r, l, False, first)
            for h in range(height):
                u = total[h]
                half = 0.5 * u
                th = jnp.tanh(u * (GELU_A + GELU_B * (u * u)))
                hid[rows(h), lane_tile(l)] = (half + half * th).astype(jnp.bfloat16)
            return carry

        lax.fori_loop(0, tiles, tile, 0)
        mixed = jnp.dot(hid[:, :chans], mix[r, :chans], preferred_element_type=jnp.float32)
        result = rx[t, r].astype(jnp.float32) + mixed.reshape(height, width, chans)
        tx[t, r] = result.astype(jnp.bfloat16)
        depart(t, r, pos + 1 - 2 * r)
        if t == ticks - 1:
            leave(r).start()

    def backward(r, t):
        pltpu.make_async_copy(stored_in.at[r, t], stored.at[r, t], stored_sem.at[r, t]).wait()
        stage(stored.at[r, t, 0, 0], xb.at[r, t])
        arrive(t, 2 + r, pos + 1 - 2 * r)

        def recompute(l, carry):
            incoming = rx[t, 2 + r].reshape(height * width, chans)
            hidden_grad[...] = lax.dot_general(
                incoming, mix[r, lane_tile(l)], (((1,), (1,)), ((), ())), preferred_element_type=jnp.float32
            )
            first = jnp.broadcast_to(kw[r, l, taps : taps + 1, :], (width, LANES))
            total = conv(xb.at[r, t, l], r, l, False, first)
            bias_sum = dk_acc[r, l, taps]
            for h in range(height):
                u = total[h]
                half = 0.5 * u
                square = u * u
                th = jnp.tanh(u * (GELU_A + GELU_B * square))
                hidb[r, t, rows(h), lane_tile(l)] = (half + half * th).astype(jnp.bfloat16)
                inner = GELU_A + (3.0 * GELU_B) * square
                slope = (0.5 + 0.5 * th) + half * (1.0 - th * th) * inner
                grad = hidden_grad[rows(h), :] * slope
                dpad[r, t, l, h, SUB : SUB + width, :] = grad
                for w in range(0, width, SUB):
                    bias_sum = bias_sum + grad[w : w + SUB]
            dk_acc[r, l, taps] = bias_sum
            return carry

        lax.fori_loop(0, tiles, recompute, 0)

        def spread(l, carry):
            total = conv(dpad.at[r, t, l], r, l, True, jnp.zeros((width, LANES), jnp.float32))
            for h in range(height):
                work[rows(h), lane_tile(l)] = total[h]
            return carry

        lax.fori_loop(0, tiles, spread, 0)
        result = rx[t, 2 + r].astype(jnp.float32) + work[:, :chans].reshape(height, width, chans)
        tx[t, 2 + r] = result.astype(jnp.bfloat16)
        if (r, t) == (1, 0):
            pl.semaphore_wait(barrier, len(greeted))
        depart(t, 2 + r, pos - 1 + 2 * r)
        if t == ticks - 1:
            leave(2 + r).start()

    def weights(r, t):
        def tile(l, carry):
            incoming = rx[t, 2 + r].reshape(height * width, chans)
            dp_acc[r, lane_tile(l), :] += lax.dot_general(
                hidb[r, t, :, lane_tile(l)], incoming, (((0,), (0,)), ((), ())), preferred_element_type=jnp.float32
            )
            grads = [dpad[r, t, l, h, SUB : SUB + width, :] for h in range(height)]
            for b in range(side):
                sums = [None] * side
                for source in range(height):
                    values = shifted(xb.at[r, t, l], source, b)
                    for a in range(side):
                        h = source - a + margin
                        if 0 <= h < height:
                            product = grads[h] * values
                            for w in range(0, width, SUB):
                                part = product[w : w + SUB]
                                sums[a] = part if sums[a] is None else sums[a] + part
                for a in range(side):
                    dk_acc[r, l, a * side + b] = dk_acc[r, l, a * side + b] + sums[a]
            return carry

        lax.fori_loop(0, tiles, tile, 0)

    def weights_of(r, start, stop):
        def one(t, carry):
            weights(r, t)
            return carry

        if stop > start:
            lax.fori_loop(start, stop, one, 0)

    def finish_small(r):
        for l, wide in enumerate(widths):
            total = jnp.sum(dk_acc[r, l], axis=1)
            small[r, : taps + 1, l * LANES : l * LANES + wide] = total[:, :wide]

    if share:
        swaps = [
            pltpu.make_async_remote_copy(
                src_ref=parcel.at[i],
                dst_ref=landed.at[i],
                send_sem=swap_send.at[i],
                recv_sem=swap_recv.at[i],
                device_id=mirror if i == 2 else peer,
                device_id_type=MESH,
            )
            for i in range(3)
        ]

    def mix_half(r, which):
        return dp_acc[r, pl.ds(pl.multiple_of(which * share, SUB), share), :]

    def small_half(r, which):
        return jnp.where(which == 0, small[r, :, :share], small[r, :, share:])

    share_whole = chans // LANES
    rest_rows = parcel_rest_rows(share, chans)
    bulk = share_whole * share
    small_rows = small.shape[1]

    def fill(i, mixed, ends):
        for l in range(share_whole):
            parcel[i, l * share : (l + 1) * share, :] = mixed[:, l * LANES : (l + 1) * LANES].astype(jnp.bfloat16)
        if rest_rows:
            for g in range(-(-share // rest_rows)):
                part = mixed[g * rest_rows : (g + 1) * rest_rows, share_whole * LANES :]
                parcel[i, bulk : bulk + part.shape[0], g * rest : (g + 1) * rest] = part.astype(jnp.bfloat16)
        for l in range(-(-share // LANES)):
            part = ends[:, l * LANES : (l + 1) * LANES]
            start = bulk + rest_rows + l * small_rows
            parcel[i, start : start + small_rows, : part.shape[1]] = part.astype(jnp.bfloat16)
        swaps[i].start()

    def opened(i):
        mixed = [landed[i, l * share : (l + 1) * share, :] for l in range(share_whole)]
        if rest_rows:
            parts = []
            for g in range(-(-share // rest_rows)):
                wanted = min(rest_rows, share - g * rest_rows)
                parts.append(landed[i, bulk : bulk + wanted, :].astype(jnp.float32)[:, g * rest : (g + 1) * rest])
            mixed.append(jnp.concatenate(parts, axis=0))
        ends = []
        for l in range(-(-share // LANES)):
            start = bulk + rest_rows + l * small_rows
            ends.append(landed[i, start : start + small_rows, : min(LANES, share - l * LANES)])
        return tuple(
            jnp.concatenate([x.astype(jnp.float32) for x in parts], axis=1) for parts in (mixed, ends)
        )

    def send_half(r):
        finish_small(r)
        fill(r, mix_half(r, 1 - half), small_half(r, 1 - half))

    def send_mirror():
        swaps[1].wait_recv()
        mixed, ends = opened(1)
        fill(2, mix_half(1, half) + mixed, small_half(1, half) + ends)

    last = ticks - 1
    for t in range(last):
        backward(1, t)
        forward(0, t)
        forward(1, t)
        if t:
            weights(1, t - 1)
        backward(0, t)
    if last:
        weights(1, last - 1)
    backward(1, last)
    weights(1, last)
    if share:
        send_half(1)
    weights_of(0, 0, last)
    if share:
        send_mirror()
    backward(0, last)
    weights(0, last)
    if share:
        send_half(0)
    forward(0, last)
    forward(1, last)

    for t in range(ticks - 1):
        for c, step in ((0, 1), (1, -1), (2, -1), (3, 1)):
            @pl.when(inside(pos + step))
            def _():
                link(t, c, pos + step).wait_send()
    if share:
        gm_out, gk_out, gb_out = outs[2:]
        swaps[0].wait_recv()
        swaps[2].wait_recv()
        near, far = opened(0), opened(2)
        gm_out[0, 0] = (mix_half(0, half) + near[0] + far[0]) * factor
        ends = (small_half(0, half) + near[1] + far[1]) * factor
        for a in range(side):
            for b in range(side):
                gk_out[0, a, b] = ends[a * side + b : a * side + b + 1]
        gb_out[0] = ends[taps : taps + 1]
        for swap in swaps:
            swap.wait_send()
    else:
        for r in range(2):
            finish_small(r)
        outs[2][...] = dp_acc[:, :chans]
        outs[3][...] = small[...]
    for c in range(4):
        leave(c).wait()


def place_kernel(*refs):
    half = len(refs) // 3
    sources, targets, held = refs[:half], refs[half : 2 * half], refs[2 * half : 3 * half]
    in_sem, out_sem = refs[3 * half :]
    trips = []
    for trio in zip(sources, held, targets):
        for source, stop, target in [[x.at[r] for x in trio] for r in range(2)] if trio[0].shape[0] == 2 else [trio]:
            i = len(trips)
            trips.append(
                (
                    pltpu.make_async_copy(source, stop, in_sem.at[i]),
                    pltpu.make_async_copy(stop, target, out_sem.at[i]),
                )
            )
    for fetch, _ in trips:
        fetch.start()
    for fetch, put in trips:
        fetch.wait()
        put.start()
    for _, put in trips:
        put.wait()


def place(results):
    anywhere = pl.BlockSpec(memory_space=pl.ANY)
    return pl.pallas_call(
        place_kernel,
        out_shape=tuple(jax.ShapeDtypeStruct(x.shape, x.dtype) for x in results),
        in_specs=[anywhere] * len(results),
        out_specs=tuple(anywhere for _ in results),
        scratch_shapes=[
            *(pltpu.VMEM(x.shape, x.dtype) for x in results),
            pltpu.SemaphoreType.DMA((2 * len(results),)),
            pltpu.SemaphoreType.DMA((2 * len(results),)),
        ],
        compiler_params=pltpu.CompilerParams(vmem_limit_bytes=60 * 1024 * 1024),
        name="place",
    )(*results)


def fold_groups(chans, height):
    rest = chans % LANES
    groups = LANES // rest if rest else 1
    return groups if height % groups == 0 else 1


def parcel_rest_rows(share, chans):
    rest = chans % LANES
    if not rest:
        return 0
    return -(-share // (LANES // rest * 16)) * 16


def relay(n, share, factor, act, cot, new_in, loss, stored, kern, bias, mix):
    ticks = stored.shape[1]
    height, width, chans = stored.shape[-3:]
    side = kern.shape[2]
    taps = side * side
    tiles = -(-chans // LANES)
    padded = tiles * LANES
    count = height * width
    across = width + 2 * SUB
    f32, bf16 = jnp.float32, jnp.bfloat16
    vmem = pl.BlockSpec(memory_space=pltpu.VMEM)
    anywhere = pl.BlockSpec(memory_space=pl.ANY)
    small = -(-(taps + 1) // 16) * 16
    mail = chans // LANES * count
    if chans % LANES:
        mail += count // fold_groups(chans, height)
    parcel = chans // LANES * share + parcel_rest_rows(share, chans) + -(-share // LANES) * small
    if share:
        sums = [(1, 1, share, chans), (1, side, side, 1, share), (1, 1, share)]
    else:
        sums = [(2, chans, chans), (2, small, chans)]
    return pl.pallas_call(
        functools.partial(relay_kernel, n, share, factor),
        out_shape=(
            jax.ShapeDtypeStruct(act.shape, bf16),
            jax.ShapeDtypeStruct(cot.shape, bf16),
            *(jax.ShapeDtypeStruct(shape, f32) for shape in sums),
        ),
        in_specs=[anywhere] * 8,
        out_specs=(anywhere, anywhere, *(vmem for _ in sums)),
        scratch_shapes=[
            pltpu.VMEM((tiles, height, across, LANES), f32),
            pltpu.VMEM((2, ticks, tiles, height, across, LANES), f32),
            pltpu.VMEM((2, ticks, tiles, height, across, LANES), f32),
            pltpu.VMEM((count, padded), bf16),
            pltpu.VMEM((2, ticks, count, padded), bf16),
            pltpu.VMEM((count, LANES), f32),
            pltpu.VMEM((count, padded), f32),
            pltpu.VMEM((2, tiles, small, LANES), f32),
            pltpu.VMEM((2, tiles, taps + 1, SUB, LANES), f32),
            pltpu.VMEM((2, padded, chans), f32),
            pltpu.VMEM((2, small, chans), f32),
            pltpu.VMEM((ticks, 4, height, width, chans), bf16),
            pltpu.VMEM((ticks, 4, height, width, chans), bf16),
            pltpu.VMEM((max(ticks - 1, 1), 4, mail, LANES), bf16),
            pltpu.VMEM((max(ticks - 1, 1), 4, mail, LANES), bf16),
            pltpu.VMEM(stored.shape, bf16),
            pltpu.VMEM(kern.shape, bf16),
            pltpu.VMEM(bias.shape, f32),
            pltpu.VMEM((2, padded, chans), bf16),
            pltpu.VMEM((3, parcel, LANES), bf16),
            pltpu.VMEM((3, parcel, LANES), bf16),
            pltpu.SemaphoreType.DMA((ticks, 4)),
            pltpu.SemaphoreType.DMA((ticks, 4)),
            pltpu.SemaphoreType.DMA((ticks, 4)),
            pltpu.SemaphoreType.DMA((4,)),
            pltpu.SemaphoreType.DMA((3,)),
            pltpu.SemaphoreType.DMA((2, ticks)),
            pltpu.SemaphoreType.DMA((3,)),
            pltpu.SemaphoreType.DMA((3,)),
        ],
        compiler_params=pltpu.CompilerParams(
            collective_id=0, has_side_effects=True, vmem_limit_bytes=60 * 1024 * 1024
        ),
        name="relay",
    )(act, cot, new_in, loss, stored, kern, bias, mix)


def per_device(
    activations, stored_inputs, cotangents, new_inputs, loss_grad, depth_kernel, depth_bias, mixing
):
    sections = lax.axis_size("section")
    copies = lax.axis_size("dp")
    side = depth_kernel.shape[-2]
    taps = side * side
    ticks = stored_inputs.shape[1]
    chans = mixing.shape[-1]
    map_rows = activations.shape[3] * activations.shape[4]
    factor = (2.0 * ticks * activations.shape[2] * copies * map_rows) ** (-0.5)
    in_kernel = copies == 2 and sections % 2 == 0 and chans % 32 == 0
    share = chans // 2 if in_kernel else 0
    outputs, grads, *sums = relay(
        sections, share, factor, activations, cotangents, new_inputs, loss_grad,
        stored_inputs, depth_kernel.transpose(0, 2, 3, 4, 1, 5), depth_bias, mixing,
    )
    if in_kernel:
        outputs, grads, grad_mixing, grad_kernel, grad_bias = place((outputs, grads, *sums))
        return (outputs, grads, grad_kernel.transpose(0, 3, 1, 2, 4), grad_bias, grad_mixing)
    mix_share = lax.psum_scatter(sums[0], "dp", scatter_dimension=1, tiled=True)
    small_share = lax.psum_scatter(sums[1], "dp", scatter_dimension=2, tiled=True)
    swap = [(i, sections - 1 - i) for i in range(sections)]
    mix_other, small_other = lax.ppermute((mix_share[1], small_share[1]), "section", swap)
    grad_mixing = ((mix_share[0] + mix_other) * factor)[None, None]
    small = (small_share[0] + small_other) * factor
    grad_kernel = small[:taps].reshape(1, 1, side, side, -1)
    grad_bias = small[taps][None, None]
    return (outputs, grads, grad_kernel, grad_bias, grad_mixing)


def solution(mesh):
    return jax.shard_map(
        per_device,
        mesh=mesh,
        in_specs=(
            P(None, "section", "dp", None, None, None),
            P(None, None, "section", "dp", None, None, None),
            P(None, "section", "dp", None, None, None),
            P(None, None, "dp", None, None, None),
            P(None, None, "dp", None, None, None),
            P("section", None, None, None, None, None),
            P("section", None, None, None),
            P("section", None, None, None, None),
        ),
        out_specs=(
            P(None, "section", "dp", None, None, None),
            P(None, "section", "dp", None, None, None),
            P("section", None, None, None, "dp"),
            P("section", None, "dp"),
            P("section", None, "dp", None),
        ),
        check_vma=False,
    )
```
